32 devices in a mesh: groups: 2 (over y), gz: 4 (over z), ta: 2 (over x), col: 2 (over core).
Axes of the slice: x: 2, y: 2, z: 4, core: 2. Of those that a mesh axis runs over, the one named last changes fastest.
Arguments:
- field: bfloat16 [64, 24, 20, 64, 128], P(('groups', 'gz'), 'ta', None, 'col'), parts along dimension 0, may hold values from -6 to 6
- cotangent: bfloat16 [64, 24, 20, 64, 128], P(('groups', 'gz'), 'ta', None, 'col'), parts along dimension 0, may hold values from -6 to 6
- spectral_weight: bfloat16 [16, 12, 576, 2, 20, 20], P('ta', None, ('gz', 'col')), may hold values from -4.1875 to 4.1875
- point_weight: bfloat16 [20, 20], replicated, may hold values from -1.25 to 1.25
- point_bias: float32 [20], replicated, may hold values from -3 to 3
Outputs:
- input_grad: bfloat16 [64, 24, 20, 64, 128], P(('groups', 'gz'), 'ta', None, 'col'), parts along dimension 0
- weight_grad: bfloat16 [32, 12, 576, 2, 20, 20], P(('groups', 'ta'), None, ('gz', 'col')), parts along dimension 0
The draws below stay inside these ranges and needn't reach their ends.
There are 2 independent parts, one for each index of `groups`. The reference program is written for one: setup_inputs(seed, part) draws one part's arguments, and reference() takes and returns one part's arrays. A program takes and returns all parts, laid end to end along the dimension named above; an argument that names none is the same for every part. Nothing has to cross between parts.
All inputs are finite; a program needn't handle non-finite values.
Results may differ from the reference program's by a relative error of at most 0.025.
Values may be sent and summed in bfloat16 or wider, within the bound.
No kernel may reach another device: no remote copies, remote signals or barrier semaphores. Data moves between devices by JAX's collectives and lax.ppermute only.
A program may use at most 384 MiB of HBM per device.

```python
import math
import jax
import jax.numpy as jnp
from jax import lax

LX = 128
LY = 64
LZ = 32
LT = 24
WIDTH = 20
MX = 24
MY = 24
MZ = 16
MT = 12
PAIRS = 576


def shard_levels(rng, dims, shards, low, high):
    factor_of, own = 1.0, jax.random.fold_in(rng, 6)
    for dim, parts in shards:
        steps = jnp.exp(jax.random.uniform(jax.random.fold_in(own, dim), (parts,), jnp.float32, low / len(shards), high / len(shards)))
        factor_of = factor_of * jnp.repeat(steps, dims[dim] // parts).reshape([-1 if axis == dim else 1 for axis in range(len(dims))])
    return factor_of


def normal_values(key, shape, deviation, limit, split=(), held_as=jnp.bfloat16):
    drawn = jax.random.normal(key, shape, jnp.float32) * deviation
    if len(split) > 0:
        drawn = shard_levels(key, shape, split, -0.22, 0.18) * drawn
    return jnp.clip(drawn, min=-limit, max=limit).astype(held_as)


def setup_inputs(seed: int = 0, part: int = 0) -> dict:
    keys = jax.random.split(jax.random.key(seed), 6)
    part_keys = jax.random.split(jax.random.fold_in(keys[5], part), 6)
    field = normal_values(part_keys[0], (LZ, LT, WIDTH, LY, LX), 1.0, 6.0, ((0, 4), (1, 2), (3, 2)))
    cotangent = normal_values(part_keys[1], (LZ, LT, WIDTH, LY, LX), 1.0, 6.0, ((0, 4), (1, 2), (3, 2)))
    spectral_weight = normal_values(keys[2], (MZ, MT, PAIRS, 2, WIDTH, WIDTH), 0.7, 4.1875, ((0, 2), (2, 8)))
    point_weight = normal_values(keys[3], (WIDTH, WIDTH), WIDTH ** -0.5, 1.25)
    point_bias = normal_values(keys[4], (WIDTH,), 0.5, 3.0, (), jnp.float32)
    return dict(field=field, cotangent=cotangent, spectral_weight=spectral_weight, point_weight=point_weight, point_bias=point_bias)


def wave_parts(length, mode_count, halfband):
    mode_index = jnp.arange(mode_count, dtype=jnp.int32)
    if halfband:
        frequency = mode_index
    else:
        frequency = jnp.where(mode_index < mode_count // 2, mode_index, mode_index - mode_count)
    places = jnp.arange(length, dtype=jnp.int32)
    phase_turns = places[:, None] * frequency[None, :] % length
    angles = phase_turns.astype(jnp.float32) * (2.0 * math.pi / length)
    scaling = 1.0 / math.sqrt(length)
    return (jnp.cos(angles) * scaling, jnp.sin(angles) * scaling)

def complex_table(length, mode_count, halfband, doubled, inverse):
    cosine, sine_part = wave_parts(length, mode_count, halfband)
    if doubled:
        factor = jnp.where(jnp.arange(mode_count) == 0, 1.0, 2.0).astype(jnp.float32)
        cosine = cosine * factor[None, :]
        sine_part = sine_part * factor[None, :]
    if inverse:
        table_out = jnp.stack([jnp.stack([cosine, sine_part], -1), jnp.stack([-sine_part, cosine], -1)], 2)
        return jnp.transpose(table_out, (1, 0, 2, 3)).astype(jnp.bfloat16)
    table_out = jnp.stack([jnp.stack([cosine, -sine_part], -1), jnp.stack([sine_part, cosine], -1)], 2)
    return table_out.astype(jnp.bfloat16)

def real_tables(length, mode_count):
    cosine, sine_part = wave_parts(length, mode_count, False)
    forward = jnp.stack([cosine, -sine_part], -1).astype(jnp.bfloat16)
    return (forward, jnp.transpose(forward, (1, 2, 0)))

def product(pattern, first_op, second_op):
    return jnp.einsum(pattern, first_op.astype(jnp.float32), second_op.astype(jnp.float32))

def analysis(field_in, x_fwd, y_fwd, z_fwd, t_fwd):
    along_x = product('ztcyx,xkr->ztcykr', field_in, x_fwd).astype(jnp.bfloat16)
    along_y = product('ztcykr,ybrs->ztcbks', along_x, y_fwd).astype(jnp.bfloat16)
    paired = along_y.reshape(LZ, LT, WIDTH, PAIRS, 2)
    along_z = product('ztcmr,zkrs->ktcms', paired, z_fwd).astype(jnp.bfloat16)
    return product('ktcmr,tqrs->kqcms', along_z, t_fwd).astype(jnp.bfloat16)

def synthesis(spectrum_in, x_inv, y_inv, z_inv, t_inv):
    along_t = product('kqomr,qtrs->ktoms', spectrum_in, t_inv).astype(jnp.bfloat16)
    along_z = product('ktomr,kzrs->ztoms', along_t, z_inv).astype(jnp.bfloat16)
    split_pairs = along_z.reshape(LZ, LT, WIDTH, MY, MX, 2)
    along_y = product('ztcbkr,byrs->ztcyks', split_pairs, y_inv).astype(jnp.bfloat16)
    return product('ztcykr,krx->ztcyx', along_y, x_inv)

def gelu_slope(values):
    normal_cdf = 0.5 * (1.0 + lax.erf(values / math.sqrt(2.0)))
    return normal_cdf + values * jnp.exp(-0.5 * values * values) / math.sqrt(2.0 * math.pi)

def reference(field, cotangent, spectral_weight, point_weight, point_bias):
    x_fwd, x_inv = real_tables(LX, MX)
    y_fwd = complex_table(LY, MY, False, False, False)
    y_inv = complex_table(LY, MY, False, False, True)
    z_fwd = complex_table(LZ, MZ, False, False, False)
    z_inv = complex_table(LZ, MZ, False, False, True)
    t_plain_fwd = complex_table(LT, MT, True, False, False)
    t_weighted_fwd = complex_table(LT, MT, True, True, False)
    t_plain_inv = complex_table(LT, MT, True, False, True)
    t_weighted_inv = complex_table(LT, MT, True, True, True)
    spectrum = analysis(field, x_fwd, y_fwd, z_fwd, t_plain_fwd)
    real_in = spectrum[..., 0]
    imag_in = spectrum[..., 1]
    real_w = spectral_weight[:, :, :, 0]
    imag_w = spectral_weight[:, :, :, 1]
    mixed_real = product('kqim,kqmio->kqom', real_in, real_w) - product('kqim,kqmio->kqom', imag_in, imag_w)
    mixed_imag = product('kqim,kqmio->kqom', real_in, imag_w) + product('kqim,kqmio->kqom', imag_in, real_w)
    mixed = jnp.stack([mixed_real, mixed_imag], -1).astype(jnp.bfloat16)
    spectral = synthesis(mixed, x_inv, y_inv, z_inv, t_weighted_inv)
    preact = spectral + product('ztcyx,co->ztoyx', field, point_weight) + point_bias[None, None, :, None, None]
    gprime = (cotangent.astype(jnp.float32) * gelu_slope(preact)).astype(jnp.bfloat16)
    gspec = analysis(gprime, x_fwd, y_fwd, z_fwd, t_weighted_fwd)
    grad_real = gspec[..., 0]
    grad_imag = gspec[..., 1]
    weight_real = product('kqim,kqom->kqmio', real_in, grad_real) + product('kqim,kqom->kqmio', imag_in, grad_imag)
    weight_imag = product('kqim,kqom->kqmio', real_in, grad_imag) - product('kqim,kqom->kqmio', imag_in, grad_real)
    weight_grad = jnp.stack([weight_real, weight_imag], 3).astype(jnp.bfloat16)
    back_real = product('kqom,kqmio->kqim', grad_real, real_w) + product('kqom,kqmio->kqim', grad_imag, imag_w)
    back_imag = product('kqom,kqmio->kqim', grad_imag, real_w) - product('kqom,kqmio->kqim', grad_real, imag_w)
    dspec = jnp.stack([back_real, back_imag], -1).astype(jnp.bfloat16)
    back_field = synthesis(dspec, x_inv, y_inv, z_inv, t_plain_inv)
    input_grad = (back_field + product('ztoyx,co->ztcyx', gprime, point_weight)).astype(jnp.bfloat16)
    return (input_grad, weight_grad)
```

```python
import functools
import math

import jax
import jax.numpy as jnp
import ml_dtypes
import numpy as np
from jax import lax
from jax.experimental import pallas as pl
from jax.experimental.pallas import tpu as pltpu
from jax.sharding import PartitionSpec as P

LX = 128
LY = 64
LZ = 32
LT = 24
WIDTH = 20
MX = 24
MY = 24
MZ = 16
MT = 12
PAIRS = 576
LANE = 128
GROUP = 8
CHUNKS = 2


def wave_parts(length, mode_count, halfband):
    mode_index = jnp.arange(mode_count, dtype=jnp.int32)
    if halfband:
        frequency = mode_index
    else:
        frequency = jnp.where(mode_index < mode_count // 2, mode_index, mode_index - mode_count)
    places = jnp.arange(length, dtype=jnp.int32)
    phase_turns = places[:, None] * frequency[None, :] % length
    angles = phase_turns.astype(jnp.float32) * (2.0 * math.pi / length)
    scaling = 1.0 / math.sqrt(length)
    return (jnp.cos(angles) * scaling, jnp.sin(angles) * scaling)


def complex_table(length, mode_count, halfband, doubled, inverse):
    cosine, sine_part = wave_parts(length, mode_count, halfband)
    if doubled:
        factor = jnp.where(jnp.arange(mode_count) == 0, 1.0, 2.0).astype(jnp.float32)
        cosine = cosine * factor[None, :]
        sine_part = sine_part * factor[None, :]
    if inverse:
        table_out = jnp.stack(
            [jnp.stack([cosine, sine_part], -1), jnp.stack([-sine_part, cosine], -1)], 2
        )
        return jnp.transpose(table_out, (1, 0, 2, 3)).astype(jnp.bfloat16)
    table_out = jnp.stack(
        [jnp.stack([cosine, -sine_part], -1), jnp.stack([sine_part, cosine], -1)], 2
    )
    return table_out.astype(jnp.bfloat16)


def real_tables(length, mode_count):
    cosine, sine_part = wave_parts(length, mode_count, False)
    forward = jnp.stack([cosine, -sine_part], 0).astype(jnp.bfloat16)
    x_forward = jnp.transpose(forward, (1, 0, 2)).reshape(length, 2 * mode_count)
    x_inverse = jnp.transpose(forward, (0, 2, 1)).reshape(2 * mode_count, length)
    return (x_forward, x_inverse)


def product(pattern, first_op, second_op):
    return jnp.einsum(pattern, first_op, second_op, preferred_element_type=jnp.float32)


def gelu_slope(values):
    normal_cdf = 0.5 * (1.0 + lax.erf(values / math.sqrt(2.0)))
    return normal_cdf + values * jnp.exp(-0.5 * values * values) / math.sqrt(2.0 * math.pi)


def general_device(field, cotangent, spectral_weight, point_weight, point_bias):
    col_index = lax.axis_index("col")
    gz_count = lax.axis_size("gz")
    col_count = lax.axis_size("col")
    depth = field.shape[0]
    steps_here = field.shape[1]
    row_count = field.shape[3]
    owners = gz_count * col_count
    owned_pairs = PAIRS // owners
    x_fwd, x_inv = real_tables(LX, MX)
    y_fwd = lax.dynamic_slice_in_dim(
        complex_table(LY, MY, False, False, False), col_index * row_count, row_count, 0
    )
    y_inv = lax.dynamic_slice_in_dim(
        complex_table(LY, MY, False, False, True), col_index * row_count, row_count, 1
    )
    z_fwd = complex_table(LZ, MZ, False, False, False)
    z_inv = complex_table(LZ, MZ, False, False, True)
    t_plain_fwd = complex_table(LT, MT, True, False, False)
    t_weighted_fwd = complex_table(LT, MT, True, True, False)
    t_plain_inv = complex_table(LT, MT, True, False, True)
    t_weighted_inv = complex_table(LT, MT, True, True, True)

    def analyse(field_in, t_table):
        along_x = product("ztcyx,xj->ztcyj", field_in, x_fwd).astype(jnp.bfloat16)
        along_x = along_x.reshape(depth, steps_here, WIDTH, row_count, 2, MX)
        partial_sums = product("ztcyrk,ybrs->ztcsbk", along_x, y_fwd)
        spread = partial_sums.reshape(depth, steps_here, WIDTH, 2, gz_count, col_count, owned_pairs)
        halves = lax.psum_scatter(
            spread.astype(jnp.bfloat16), "col", scatter_dimension=5, tiled=True
        )
        mine = halves.reshape(depth, steps_here, WIDTH, 2, gz_count, owned_pairs)
        moved = lax.all_to_all(mine, "gz", split_axis=4, concat_axis=0, tiled=True)
        owned = moved.reshape(LZ, steps_here, WIDTH, 2, owned_pairs)
        along_z = product("ztcrm,zkrs->ktcsm", owned, z_fwd).astype(jnp.bfloat16)
        full_time = lax.all_to_all(along_z, "ta", split_axis=0, concat_axis=1, tiled=True)
        return product("ktcrm,tqrs->kqcsm", full_time, t_table).astype(jnp.bfloat16)

    def synthesize(spectrum_in, t_table):
        along_t = product("kqorm,qtrs->ktosm", spectrum_in, t_table).astype(jnp.bfloat16)
        own_steps = lax.all_to_all(along_t, "ta", split_axis=1, concat_axis=0, tiled=True)
        along_z = product("ktorm,kzrs->ztosm", own_steps, z_inv).astype(jnp.bfloat16)
        blocks = along_z.reshape(gz_count, depth, steps_here, WIDTH, 2, owned_pairs)
        copies = jnp.broadcast_to(
            blocks[:, None], (gz_count, col_count, depth, steps_here, WIDTH, 2, owned_pairs)
        )
        copies = copies.reshape(owners, depth, steps_here, WIDTH, 2, owned_pairs)
        gathered = lax.all_to_all(copies, ("gz", "col"), split_axis=0, concat_axis=5, tiled=True)
        split_pairs = gathered.reshape(depth, steps_here, WIDTH, 2, MY, MX)
        along_y = product("ztcrbk,byrs->ztcysk", split_pairs, y_inv).astype(jnp.bfloat16)
        along_y = along_y.reshape(depth, steps_here, WIDTH, row_count, 2 * MX)
        return product("ztcyj,jx->ztcyx", along_y, x_inv)

    spectrum = analyse(field, t_plain_fwd)
    real_in = spectrum[:, :, :, 0]
    imag_in = spectrum[:, :, :, 1]
    real_w = spectral_weight[:, :, :, 0]
    imag_w = spectral_weight[:, :, :, 1]
    mixed_real = product("kqim,kqmio->kqom", real_in, real_w) - product(
        "kqim,kqmio->kqom", imag_in, imag_w
    )
    mixed_imag = product("kqim,kqmio->kqom", real_in, imag_w) + product(
        "kqim,kqmio->kqom", imag_in, real_w
    )
    mixed = jnp.stack([mixed_real, mixed_imag], 3).astype(jnp.bfloat16)
    spectral = synthesize(mixed, t_weighted_inv)
    preact = (
        spectral
        + product("ztcyx,co->ztoyx", field, point_weight)
        + point_bias[None, None, :, None, None]
    )
    gprime = (cotangent.astype(jnp.float32) * gelu_slope(preact)).astype(jnp.bfloat16)
    gspec = analyse(gprime, t_weighted_fwd)
    grad_real = gspec[:, :, :, 0]
    grad_imag = gspec[:, :, :, 1]
    weight_real = product("kqim,kqom->kqmio", real_in, grad_real) + product(
        "kqim,kqom->kqmio", imag_in, grad_imag
    )
    weight_imag = product("kqim,kqom->kqmio", real_in, grad_imag) - product(
        "kqim,kqom->kqmio", imag_in, grad_real
    )
    weight_grad = jnp.stack([weight_real, weight_imag], 3).astype(jnp.bfloat16)
    back_real = product("kqom,kqmio->kqim", grad_real, real_w) + product(
        "kqom,kqmio->kqim", grad_imag, imag_w
    )
    back_imag = product("kqom,kqmio->kqim", grad_imag, real_w) - product(
        "kqom,kqmio->kqim", grad_real, imag_w
    )
    dspec = jnp.stack([back_real, back_imag], 3).astype(jnp.bfloat16)
    back_field = synthesize(dspec, t_plain_inv)
    input_grad = (back_field + product("ztoyx,co->ztcyx", gprime, point_weight)).astype(
        jnp.bfloat16
    )
    return (input_grad, weight_grad)


def waves(length, frequencies, places):
    turns = (np.asarray(places)[:, None] * np.asarray(frequencies)[None, :]) % length
    angles = turns * (2.0 * math.pi / length)
    scaling = 1.0 / math.sqrt(length)
    return np.cos(angles) * scaling, np.sin(angles) * scaling


def signed(count):
    return [k if k < count // 2 else k - count for k in range(count)]


def bf16(table):
    return np.asarray(table, dtype=np.float32).astype(ml_dtypes.bfloat16)


class Plan:
    def __init__(self, mesh, depth, steps, rows):
        self.gz, self.ta, self.col = mesh.shape["gz"], mesh.shape["ta"], mesh.shape["col"]
        self.depth, self.steps, self.rows = depth, steps, rows
        self.owned = PAIRS // (self.gz * self.col)
        self.ky_own = self.owned // MX
        self.ky_half = MY // self.col
        self.lanes = self.ky_half * 2 * MX
        self.half_pairs = self.ky_half * MX
        self.kt = MT // self.ta
        self.kz = MZ // self.ta
        self.grid_rows = steps * WIDTH

    def y_tables(self):
        out = np.zeros((self.gz, self.col, 2 * MY * GROUP, GROUP * self.rows), np.float32)
        freq = np.array(signed(MY))
        for a in range(self.gz):
            for b in range(self.col):
                order = [
                    self.ky_own * (self.col * ((a + k) % self.gz) + (b ^ h)) + j
                    for h in range(self.col)
                    for k in range(self.gz)
                    for j in range(self.ky_own)
                ]
                places = np.arange(self.rows) + b * self.rows
                c, s = waves(LY, freq[order], places)
                part = np.stack([c.T, -s.T], 0)
                full = np.einsum("sky,gh->skghy", part, np.eye(GROUP))
                out[a, b] = full.reshape(out.shape[2:])
        return bf16(out.reshape(self.gz * self.col, *out.shape[2:]))

    def x_tiles(self):
        c, s = waves(LX, signed(MX), np.arange(LX))
        one = np.zeros((2, LX, 2, MX))
        one[0, :, 0], one[1, :, 0], one[0, :, 1], one[1, :, 1] = c, s, -s, c
        one = one.reshape(2 * LX, 2 * MX)
        tiles = []
        for low in range(0, self.lanes, 256):
            high = min(low + 256, self.lanes)
            kys = [k for k in range(self.ky_half) if k * 2 * MX < high and (k + 1) * 2 * MX > low]
            table = np.zeros((len(kys), 2 * LX, self.lanes), np.float32)
            for n, k in enumerate(kys):
                table[n, :, k * 2 * MX : (k + 1) * 2 * MX] = one
            table = table[:, :, low:high].reshape(len(kys) * 2 * LX, high - low)
            tiles.append((low, high, kys, bf16(table)))
        return tiles

    def x_windows(self):
        c, s = waves(LX, signed(MX), np.arange(LX))
        one = np.zeros((2, MX, 2, LX))
        one[0, :, 0], one[1, :, 0], one[0, :, 1], one[1, :, 1] = c.T, -s.T, s.T, c.T
        one = one.reshape(2 * MX, 2 * LX)
        windows, table = [], np.zeros((self.ky_half, 256, 2 * LX), np.float32)
        for k in range(self.ky_half):
            low = k * 2 * MX // 128 * 128
            high = min(low + 256, self.lanes)
            table[k, k * 2 * MX - low : (k + 1) * 2 * MX - low] = one
            windows.append((low, high))
        return windows, bf16(table)

    def t_tables(self, weighted):
        weight = np.array([1.0] + [2.0] * (MT - 1)) if weighted else np.ones(MT)
        gp = self.grid_rows_padded()
        eye = np.eye(WIDTH)
        fwd = np.zeros((self.ta, self.grid_rows, 2, self.ta, LANE), np.float32)
        inv = np.zeros((self.ta, self.ta, 2, LANE, 2, gp), np.float32)
        for a in range(self.ta):
            c, s = waves(LT, np.arange(MT), np.arange(self.steps) + a * self.steps)
            c, s = bf16(c * weight).astype(np.float32), bf16(s * weight).astype(np.float32)
            for h in range(self.ta):
                pick = slice((a ^ h) * self.kt, ((a ^ h) + 1) * self.kt)
                n = self.kt * WIDTH
                kc = np.einsum("tk,cd->tckd", c[:, pick], eye).reshape(self.grid_rows, n)
                ks = np.einsum("tk,cd->tckd", s[:, pick], eye).reshape(self.grid_rows, n)
                fwd[a, :, 0, h, :n], fwd[a, :, 1, h, :n] = kc, -ks
                g = self.grid_rows
                inv[a, h, 0, :n, 0, :g], inv[a, h, 1, :n, 0, :g] = kc.T, -ks.T
                inv[a, h, 0, :n, 1, :g], inv[a, h, 1, :n, 1, :g] = ks.T, kc.T
        fwd = fwd.reshape(self.ta, self.grid_rows, 2 * self.ta * LANE)
        return bf16(fwd), bf16(inv.reshape(self.ta, self.ta * 2 * LANE, 2 * gp))

    def grid_rows_padded(self):
        return (self.grid_rows + LANE - 1) // LANE * LANE

    def z_tables(self):
        shape = (self.ta, 2, self.kz, 2, self.gz, self.depth)
        fwd = np.zeros((self.gz, self.ta) + shape, np.float32)
        inv = np.zeros_like(fwd)
        freq = np.array(signed(MZ))
        for a in range(self.gz):
            places = np.concatenate(
                [np.arange(self.depth) + (a - k) % self.gz * self.depth for k in range(self.gz)]
            )
            for b in range(self.ta):
                for h in range(self.ta):
                    own = freq[(b ^ h) * self.kz : ((b ^ h) + 1) * self.kz]
                    c, s = waves(LZ, own, places)
                    c, s = (v.T.reshape(self.kz, self.gz, self.depth) for v in (c, s))
                    f, i = fwd[a, b, h], inv[a, b, h]
                    f[0, :, 0], f[0, :, 1], f[1, :, 0], f[1, :, 1] = c, s, -s, c
                    i[0, :, 0], i[0, :, 1], i[1, :, 0], i[1, :, 1] = c, s, -s, c
        eye = np.eye(GROUP)
        n = self.gz * self.ta
        f = np.einsum("abhskrmz,pq->abhskprmzq", fwd, eye)
        i = np.einsum("abhskrmz,pq->abrmzphskq", inv, eye)
        rows = self.ta * 2 * self.kz * GROUP
        cols = 2 * self.gz * self.depth * GROUP
        return bf16(f.reshape(n, rows, cols)), bf16(i.reshape(n, cols, rows))

    def pair_rows(self):
        n = self.kt * WIDTH
        table = np.zeros((self.ta, n, 2, self.ta, 2, LANE), np.float32)
        for h in range(self.ta):
            for r in range(2):
                table[h, np.arange(n), r, h, r, np.arange(n)] = 1.0
        return bf16(table.reshape(self.ta * n * 2, self.ta * 2 * LANE))


def dot(a, b):
    return jnp.dot(a, b, preferred_element_type=jnp.float32)


def dot_nt(a, b):
    return lax.dot_general(a, b, (((1,), (1,)), ((), ())), preferred_element_type=jnp.float32)


def slope_of(v):
    e = jnp.exp(-0.5 * v * v)
    t = 1.0 / (1.0 + (0.3275911 / math.sqrt(2.0)) * jnp.abs(v))
    poly = t * (
        0.5 * 0.254829592
        + t
        * (
            0.5 * -0.284496736
            + t * (0.5 * 1.421413741 + t * (0.5 * -1.453152027 + t * (0.5 * 1.061405429)))
        )
    )
    tail = poly * e
    cdf = jnp.where(v >= 0.0, 1.0 - tail, tail)
    return cdf + v * e * (1.0 / math.sqrt(2.0 * math.pi))


def params(steps=1):
    return pltpu.CompilerParams(
        vmem_limit_bytes=56 << 20, dimension_semantics=("arbitrary",) * steps
    )


def whole_block(a):
    return pl.BlockSpec(a.shape, lambda *i, n=a.ndim: (0,) * n)


def spread_y(plan, fields, base, count, ty, us):
    for q in range(count // (2 * GROUP)):
        g = pl.multiple_of(base + q * 2 * GROUP, 2 * GROUP)
        a = fields[0, pl.ds(g, GROUP)].reshape(GROUP * plan.rows, LX)
        b = fields[0, pl.ds(g + GROUP, GROUP)].reshape(GROUP * plan.rows, LX)
        u = dot(ty, jnp.concatenate([a, b], 1))
        ua = u[:, :LX].reshape(2 * MY, GROUP, LX)
        ub = u[:, LX:].reshape(2 * MY, GROUP, LX)
        us[:, pl.ds(g, 2 * GROUP), :] = jnp.concatenate([ua, ub], 1).astype(jnp.bfloat16)


def gather_x(plan, tiles, us, tables, outs):
    for h in range(plan.col):
        for (low, high, kys, _), table in zip(tiles, tables):
            parts = []
            for k in kys:
                ky = h * plan.ky_half + k
                parts += [us[ky], us[MY + ky]]
            o = dot(jnp.concatenate(parts, 1), table[...])
            outs[h][0, :, low:high] = o.astype(jnp.bfloat16)


def rows_call(kernel, n, plan, grid, inputs, specs, out_shapes, out_specs, scratch, aliases, flops):
    size = sum(math.prod(s.shape) * 2 for s in out_shapes)
    return pl.pallas_call(
        kernel,
        grid=(grid,),
        in_specs=specs,
        out_specs=out_specs,
        out_shape=out_shapes,
        scratch_shapes=scratch,
        input_output_aliases=aliases,
        compiler_params=params(),
        name=n,
        cost_estimate=pl.CostEstimate(
            flops=int(flops), bytes_accessed=int(size * 2), transcendentals=0
        ),
    )(*inputs)


def analyse_xy(plan, tiles, field, ty, z0, zc):
    def kernel(f, ty_ref, *refs):
        tables, outs, us = refs[: len(tiles)], refs[len(tiles) : -1], refs[-1]
        step = 5 * 2 * GROUP
        def body(i, carry):
            spread_y(plan, f, i * step, step, ty_ref[...], us)
            return carry
        lax.fori_loop(0, plan.grid_rows // step, body, 0)
        gather_x(plan, tiles, us, tables, outs)

    tabs = [jnp.asarray(t[3]) for t in tiles]
    out = jax.ShapeDtypeStruct((zc, plan.grid_rows, plan.lanes), jnp.bfloat16)
    block = pl.BlockSpec((1, plan.grid_rows, plan.lanes), lambda z: (z, 0, 0))
    fspec = pl.BlockSpec((1, plan.grid_rows, plan.rows, LX), lambda z: (z0 + z, 0, 0, 0))
    return rows_call(
        kernel, "analyse_xy", plan, zc, [field, ty, *tabs],
        [fspec, whole_block(ty)] + [whole_block(t) for t in tabs],
        [out, out], [block, block],
        [pltpu.VMEM((2 * MY, plan.grid_rows, LX), jnp.bfloat16)], {}, zc * 24e9,
    )


def field_pass(plan, tiles, windows, own, other, field, mixer, ty, ty_inv, xi, z0, zc, cot=None, bias=None, full=None):
    first = cot is not None
    tabs = [jnp.asarray(t[3]) for t in tiles] if first else []
    block_rows = 4 * WIDTH
    half = plan.rows // 2

    def kernel(*refs):
        refs = list(refs)
        s_refs = (refs.pop(0), refs.pop(0))
        f, mix, tyi, xi_ref = refs.pop(0), refs.pop(0), refs.pop(0), refs.pop(0)
        if first:
            c_ref, bias_ref, ty_ref = refs.pop(0), refs.pop(0), refs.pop(0)
            tables = [refs.pop(0) for _ in tabs]
            g_out = refs.pop(0)
            outs = (refs.pop(0), refs.pop(0))
            us = refs.pop()
        else:
            if full is not None:
                refs.pop(0)
            g_out = refs.pop(0)
        ws, pre = refs
        for h in range(plan.col):
            for k in range(plan.ky_half):
                low, high = windows[k]
                w = dot(s_refs[h][0, :, low:high], xi_ref[k, : high - low])
                ws[h * plan.ky_half + k] = w[:, :LX]
                ws[MY + h * plan.ky_half + k] = w[:, LX:]

        def block(i, carry):
            base = pl.multiple_of(i * block_rows, block_rows)
            for q in range(block_rows // (2 * GROUP)):
                g = pl.multiple_of(base + q * 2 * GROUP, GROUP)
                a = ws[:, pl.ds(g, GROUP), :].reshape(2 * MY * GROUP, LX).astype(jnp.bfloat16)
                b = ws[:, pl.ds(g + GROUP, GROUP), :].reshape(2 * MY * GROUP, LX).astype(jnp.bfloat16)
                o = dot(tyi[...], jnp.concatenate([a, b], 1))
                at = q * 2 * GROUP
                pre[at : at + GROUP] = o[:, :LX].reshape(GROUP, plan.rows, LX)
                pre[at + GROUP : at + 2 * GROUP] = o[:, LX:].reshape(GROUP, plan.rows, LX)
            for t in range(block_rows // WIDTH):
                v = f[0, pl.ds(base + t * WIDTH, WIDTH)]
                a = v[:, :half].reshape(WIDTH * half, LX)
                b = v[:, half:].reshape(WIDTH * half, LX)
                o = dot(mix[...], jnp.concatenate([a, b], 1))
                at = t * WIDTH
                pre[at : at + WIDTH, :half] += o[:, :LX].reshape(WIDTH, half, LX)
                pre[at : at + WIDTH, half:] += o[:, LX:].reshape(WIDTH, half, LX)
            if first:
                def slopes(j, c2):
                    for m in range(4):
                        v = pre[j * 4 + m] + bias_ref[lax.rem(j * 4 + m, WIDTH)]
                        c = c_ref[0, base + j * 4 + m].astype(jnp.float32)
                        g_out[0, base + j * 4 + m] = (c * slope_of(v)).astype(jnp.bfloat16)
                    return c2
                lax.fori_loop(0, block_rows // 4, slopes, 0)
                spread_y(plan, g_out, base, block_rows, ty_ref[...], us)
            else:
                g_out[0, pl.ds(base, block_rows)] = pre[...].astype(jnp.bfloat16)
            return carry

        lax.fori_loop(0, plan.grid_rows // block_rows, block, 0)
        if first:
            gather_x(plan, tiles, us, tables, outs)

    cell = (1, plan.grid_rows, plan.rows, LX)
    local = pl.BlockSpec(cell, lambda z: (z, 0, 0, 0))
    placed = pl.BlockSpec(cell, lambda z: (z0 + z, 0, 0, 0))
    sblock = pl.BlockSpec((1, plan.grid_rows, plan.lanes), lambda z: (z, 0, 0))
    scratch = [
        pltpu.VMEM((2 * MY, plan.grid_rows, LX), jnp.float32),
        pltpu.VMEM((block_rows, plan.rows, LX), jnp.float32),
    ]
    if first:
        inputs = [own, other, field, mixer, ty_inv, xi, cot, bias, ty, *tabs]
        specs = [sblock, sblock, placed, whole_block(mixer), whole_block(ty_inv), whole_block(xi), placed]
        specs += [pl.BlockSpec(memory_space=pltpu.SMEM), whole_block(ty)] + [whole_block(t) for t in tabs]
        spec = jax.ShapeDtypeStruct((zc, plan.grid_rows, plan.lanes), jnp.bfloat16)
        gout = jax.ShapeDtypeStruct((zc,) + cell[1:], jnp.bfloat16)
        return rows_call(
            kernel, "slope_pass", plan, zc, inputs, specs, [gout, spec, spec], [local, sblock, sblock],
            scratch + [pltpu.VMEM((2 * MY, plan.grid_rows, LX), jnp.bfloat16)], {}, zc * 70e9,
        )
    inputs = [own, other, field, mixer, ty_inv, xi]
    specs = [sblock, sblock, local, whole_block(mixer), whole_block(ty_inv), whole_block(xi)]
    aliases = {}
    if full is not None:
        aliases = {len(inputs): 0}
        inputs.append(full)
        specs.append(pl.BlockSpec(memory_space=pl.ANY))
    gout = jax.ShapeDtypeStruct((plan.depth,) + cell[1:], jnp.bfloat16)
    return rows_call(
        kernel, "input_pass", plan, zc, inputs, specs, [gout], [placed], scratch, aliases, zc * 35e9
    )[0]


def time_forward(plan, own, other, table):
    zc = own.shape[0]
    hp = plan.half_pairs

    def kernel(a_ref, b_ref, m_ref, keep, send):
        a = a_ref[0].astype(jnp.float32) + b_ref[0].astype(jnp.float32)
        at = jnp.transpose(a).astype(jnp.bfloat16)
        p = dot(at, m_ref[...]).reshape(plan.ky_half, 2, MX, 4 * LANE)
        re = p[:, 0, :, : 2 * LANE] - p[:, 1, :, 2 * LANE :]
        im = p[:, 0, :, 2 * LANE :] + p[:, 1, :, : 2 * LANE]
        re, im = (v.reshape(plan.gz, 1, plan.owned, 2 * LANE).astype(jnp.bfloat16) for v in (re, im))
        keep[...] = jnp.concatenate([re[..., :LANE], im[..., :LANE]], -1)
        send[...] = jnp.concatenate([re[..., LANE:], im[..., LANE:]], -1)

    block = pl.BlockSpec((1, plan.grid_rows, plan.lanes), lambda z: (z, 0, 0))
    out = jax.ShapeDtypeStruct((plan.gz, zc, plan.owned, 2 * LANE), jnp.bfloat16)
    ospec = pl.BlockSpec((plan.gz, 1, plan.owned, 2 * LANE), lambda z: (0, z, 0, 0))
    return rows_call(
        kernel, "time_forward", plan, zc, [own, other, table], [block, block, whole_block(table)],
        [out, out], [ospec, ospec], [], {}, zc * 1e9,
    )


def time_inverse(plan, keep, got, table):
    zc = keep.shape[1]
    gp = plan.grid_rows_padded()

    def kernel(a_ref, b_ref, m_ref, out):
        rows = plan.half_pairs
        a = a_ref[...].reshape(rows, 2 * LANE)
        b = b_ref[...].reshape(rows, 2 * LANE)
        o = dot(jnp.concatenate([a, b], 1), m_ref[...]).reshape(plan.ky_half, 1, MX, 2 * gp)
        o = jnp.concatenate([o[..., :gp], o[..., gp:]], 1).reshape(plan.lanes, gp)
        out[0] = jnp.transpose(o)[: plan.grid_rows].astype(jnp.bfloat16)

    ispec = pl.BlockSpec((plan.gz, 1, plan.owned, 2 * LANE), lambda z: (0, z, 0, 0))
    out = jax.ShapeDtypeStruct((zc, plan.grid_rows, plan.lanes), jnp.bfloat16)
    return rows_call(
        kernel, "time_inverse", plan, zc, [keep, got, table], [ispec, ispec, whole_block(table)],
        [out], [pl.BlockSpec((1, plan.grid_rows, plan.lanes), lambda z: (z, 0, 0))], [], {}, zc * 1e9,
    )[0]


def depth_forward(plan, pieces, table):
    flat = [p for chunk in pieces for p in chunk]
    n = len(flat)
    zc = pieces[0][0].shape[0]
    octets = plan.owned // GROUP
    count = plan.gz * plan.depth

    def kernel(*refs):
        ins, m_ref, keep, send, buf, out = refs[:n], refs[n], refs[n + 1], refs[n + 2], refs[n + 3], refs[n + 4]
        for c in range(len(pieces)):
            for k in range(plan.gz):
                at = k * plan.depth + c * zc
                buf[at : at + zc] = ins[c * plan.gz + k][...].astype(jnp.float32)
        for o in range(octets):
            x = buf[:, o * GROUP : (o + 1) * GROUP, :].reshape(count * GROUP, 2 * LANE)
            x = jnp.concatenate([x[:, :LANE], x[:, LANE:]], 0).astype(jnp.bfloat16)
            y = dot(m_ref[...], x).reshape(plan.ta, 2, plan.kz, GROUP, LANE)
            for h in range(plan.ta):
                for s in range(2):
                    out[h, :, o * GROUP : (o + 1) * GROUP, s * LANE : (s + 1) * LANE] = y[h, s]
        keep[...] = out[0].astype(jnp.bfloat16)
        send[...] = out[1].astype(jnp.bfloat16)

    shape = jax.ShapeDtypeStruct((plan.kz, plan.owned, 2 * LANE), jnp.bfloat16)
    return rows_call(
        kernel, "depth_forward", plan, 1, [*flat, table], [whole_block(a) for a in flat] + [whole_block(table)],
        [shape, shape], [pl.BlockSpec(shape.shape, lambda i: (0, 0, 0))] * 2,
        [
            pltpu.VMEM((count, plan.owned, 2 * LANE), jnp.float32),
            pltpu.VMEM((plan.ta, plan.kz, plan.owned, 2 * LANE), jnp.float32),
        ], {}, 1e9,
    )


def depth_inverse(plan, keep, got, table, chunks):
    octets = plan.owned // GROUP
    zc = plan.depth // chunks
    count = plan.gz * plan.depth

    def kernel(a_ref, b_ref, m_ref, *refs):
        outs, buf, out = refs[:-2], refs[-2], refs[-1]
        buf[0] = a_ref[...].astype(jnp.float32)
        buf[1] = b_ref[...].astype(jnp.float32)
        for o in range(octets):
            rows = slice(o * GROUP, (o + 1) * GROUP)
            x = [
                buf[h, :, rows, s * LANE : (s + 1) * LANE].reshape(plan.kz * GROUP, LANE)
                for h in range(plan.ta)
                for s in range(2)
            ]
            y = dot(m_ref[...], jnp.concatenate(x, 0).astype(jnp.bfloat16))
            y = y.reshape(2, count, GROUP, LANE)
            for s in range(2):
                out[:, rows, s * LANE : (s + 1) * LANE] = y[s]
        for c in range(chunks):
            for k in range(plan.gz):
                at = k * plan.depth + c * zc
                outs[c * plan.gz + k][...] = out[at : at + zc].astype(jnp.bfloat16)

    shape = jax.ShapeDtypeStruct((zc, plan.owned, 2 * LANE), jnp.bfloat16)
    n = chunks * plan.gz
    flat = rows_call(
        kernel, "depth_inverse", plan, 1, [keep, got, table],
        [whole_block(keep), whole_block(got), whole_block(table)],
        [shape] * n, [pl.BlockSpec(shape.shape, lambda i: (0, 0, 0))] * n,
        [
            pltpu.VMEM((plan.ta, plan.kz, plan.owned, 2 * LANE), jnp.float32),
            pltpu.VMEM((count, plan.owned, 2 * LANE), jnp.float32),
        ], {}, 1e9,
    )
    return [flat[c * plan.gz : (c + 1) * plan.gz] for c in range(chunks)]


def swap_pairs(v):
    n = v.shape[0]
    even = lax.rem(lax.broadcasted_iota(jnp.int32, v.shape, 0), 2) == 0
    return jnp.where(even, -pltpu.roll(v, n - 1, 0), pltpu.roll(v, 1, 0))


def to_comm(plan, rows_ref, perm, keep, send):
    flat = rows_ref[...].astype(jnp.bfloat16)
    p = plan.owned
    unit = (lax.broadcasted_iota(jnp.int32, (p, p), 0) == lax.broadcasted_iota(jnp.int32, (p, p), 1))
    turned = dot_nt(unit.astype(jnp.bfloat16), flat).astype(jnp.bfloat16)
    o = dot(turned, perm[...]).astype(jnp.bfloat16)
    keep[0] = o[:, : 2 * LANE]
    send[0] = o[:, 2 * LANE :]


def mode_specs(plan):
    mode_rows = MT * WIDTH * WIDTH * 2
    half = pl.BlockSpec((1, plan.owned, 2 * LANE), lambda k: (k, 0, 0))
    weights = pl.BlockSpec((1, mode_rows, plan.owned), lambda k: (k, 0, 0))
    return half, weights, mode_rows


def mix_modes(plan, spec, weights, here, perm, unit):
    half, wspec, mode_rows = mode_specs(plan)
    per_t = WIDTH * WIDTH * 2
    wide = 2 * WIDTH

    def kernel(here_ref, a_ref, b_ref, w_ref, perm_ref, unit_ref, keep, send, xs, ms):
        x = jnp.concatenate([a_ref[0], b_ref[0]], 1)
        xs[...] = dot_nt(unit_ref[...], x)

        def step(q, carry):
            h = q // plan.kt
            kt = q - h * plan.kt
            at = lax.rem(q + here_ref[0] * plan.kt, MT)
            row = h * 2 * LANE + kt * WIDTH
            s1 = jnp.zeros((wide, plan.owned), jnp.float32)
            s2 = jnp.zeros((wide, plan.owned), jnp.float32)
            for i in range(0, WIDTH, 2):
                w = w_ref[0, pl.ds(pl.multiple_of(at * per_t + i * wide, 2 * wide), 2 * wide), :].astype(jnp.float32)
                for j in range(2):
                    wi = w[j * wide : (j + 1) * wide]
                    s1 += xs[pl.ds(row + i + j, 1), :] * wi
                    s2 += xs[pl.ds(row + LANE + i + j, 1), :] * wi
            ms[pl.ds(pl.multiple_of(q * wide, 8), wide), :] = s1 + swap_pairs(s2)
            return carry

        lax.fori_loop(0, MT, step, 0)
        to_comm(plan, ms, perm_ref, keep, send)

    shape = jax.ShapeDtypeStruct((plan.kz, plan.owned, 2 * LANE), jnp.bfloat16)
    return rows_call(
        kernel, "mix_modes", plan, plan.kz, [here, *spec, weights, perm, unit],
        [pl.BlockSpec(memory_space=pltpu.SMEM), half, half, wspec, whole_block(perm), whole_block(unit)],
        [shape, shape], [half, half],
        [
            pltpu.VMEM((2 * plan.ta * LANE, plan.owned), jnp.float32),
            pltpu.VMEM((MT * wide, plan.owned), jnp.float32),
        ], {}, 1e9,
    )


def back_modes(plan, grad, weights, here, perm):
    half, wspec, mode_rows = mode_specs(plan)
    per_t = WIDTH * WIDTH * 2
    wide = 2 * WIDTH

    def kernel(here_ref, a_ref, b_ref, w_ref, perm_ref, keep, send, gs, ms):
        gs[...] = dot_nt(perm_ref[...], jnp.concatenate([a_ref[0], b_ref[0]], 1))

        def step(q, carry):
            at = lax.rem(q + here_ref[0] * plan.kt, MT)
            g = gs[pl.ds(pl.multiple_of(q * wide, 8), wide), :]
            g2 = -swap_pairs(g)
            rows = []
            for i in range(0, WIDTH, 2):
                w = w_ref[0, pl.ds(pl.multiple_of(at * per_t + i * wide, 2 * wide), 2 * wide), :].astype(jnp.float32)
                for j in range(2):
                    wi = w[j * wide : (j + 1) * wide]
                    rows.append(jnp.sum(g * wi, 0, keepdims=True))
                    rows.append(jnp.sum(g2 * wi, 0, keepdims=True))
            ms[pl.ds(pl.multiple_of(q * wide, 8), wide), :] = jnp.concatenate(rows, 0)
            return carry

        lax.fori_loop(0, MT, step, 0)
        to_comm(plan, ms, perm_ref, keep, send)

    shape = jax.ShapeDtypeStruct((plan.kz, plan.owned, 2 * LANE), jnp.bfloat16)
    return rows_call(
        kernel, "back_modes", plan, plan.kz, [here, *grad, weights, perm],
        [pl.BlockSpec(memory_space=pltpu.SMEM), half, half, wspec, whole_block(perm)],
        [shape, shape], [half, half],
        [pltpu.VMEM((MT * wide, plan.owned), jnp.float32)] * 2, {}, 1e9,
    )


def weight_modes(plan, spec, grad, here, perm, unit):
    half, wspec, mode_rows = mode_specs(plan)
    per_t = WIDTH * WIDTH * 2
    wide = 2 * WIDTH

    def kernel(here_ref, xa, xb, ga, gb, perm_ref, unit_ref, out, xs, gs):
        xs[...] = dot_nt(unit_ref[...], jnp.concatenate([xa[0], xb[0]], 1))
        gs[...] = dot_nt(perm_ref[...], jnp.concatenate([ga[0], gb[0]], 1))

        def step(q, carry):
            h = q // plan.kt
            kt = q - h * plan.kt
            at = lax.rem(q + here_ref[0] * plan.kt, MT)
            row = h * 2 * LANE + kt * WIDTH
            g = gs[pl.ds(pl.multiple_of(q * wide, 8), wide), :]
            g2 = -swap_pairs(g)
            for i in range(0, WIDTH, 2):
                two = [
                    xs[pl.ds(row + i + j, 1), :] * g + xs[pl.ds(row + LANE + i + j, 1), :] * g2
                    for j in range(2)
                ]
                rows = pl.ds(pl.multiple_of(at * per_t + i * wide, 2 * wide), 2 * wide)
                out[0, rows, :] = jnp.concatenate(two, 0).astype(jnp.bfloat16)
            return carry

        lax.fori_loop(0, MT, step, 0)

    shape = jax.ShapeDtypeStruct((plan.kz, mode_rows, plan.owned), jnp.bfloat16)
    return rows_call(
        kernel, "weight_modes", plan, plan.kz, [here, *spec, *grad, perm, unit],
        [pl.BlockSpec(memory_space=pltpu.SMEM), half, half, half, half, whole_block(perm), whole_block(unit)],
        [shape], [wspec],
        [
            pltpu.VMEM((2 * plan.ta * LANE, plan.owned), jnp.float32),
            pltpu.VMEM((MT * wide, plan.owned), jnp.float32),
        ], {}, 1e9,
    )[0]


def direct_device(plan, field, cotangent, spectral_weight, point_weight, point_bias):
    gz_at, ta_at, col_at = (lax.axis_index(a) for a in ("gz", "ta", "col"))
    chunks = CHUNKS
    zc = plan.depth // chunks
    pick = lambda table, at: lax.dynamic_index_in_dim(jnp.asarray(table), at, 0, keepdims=False)
    ty = pick(plan.y_tables(), gz_at * plan.col + col_at)
    ty_inv = ty.T
    tiles = plan.x_tiles()
    windows, xi = plan.x_windows()
    xi = jnp.asarray(xi)
    zf, zi = plan.z_tables()
    z_at = gz_at * plan.ta + ta_at
    zf, zi = pick(zf, z_at), pick(zi, z_at)
    plain, weighted = plan.t_tables(False), plan.t_tables(True)
    perm = jnp.asarray(plan.pair_rows())
    unit = jnp.eye(2 * plan.ta * LANE, dtype=jnp.bfloat16)
    here = ta_at.astype(jnp.int32).reshape(1)
    half = plan.rows // 2
    eye = jnp.eye(half, dtype=jnp.bfloat16)
    kron = lambda m: (m[:, None, :, None] * eye[None, :, None, :]).reshape(WIDTH * half, WIDTH * half)
    mix_out, mix_in = kron(point_weight.T), kron(point_weight)
    flat = (plan.depth, plan.grid_rows, plan.rows, LX)
    field, cotangent = field.reshape(flat), cotangent.reshape(flat)
    weights = jnp.transpose(spectral_weight, (0, 1, 4, 5, 3, 2))
    weights = weights.reshape(plan.kz, MT * WIDTH * WIDTH * 2, plan.owned)

    def swap(a, axis):
        return lax.ppermute(a, axis, [(0, 1), (1, 0)])

    def shift(a, k):
        return lax.ppermute(a, "gz", [(d, (d + k) % plan.gz) for d in range(plan.gz)])

    def outward(own, other, table):
        keep, send = time_forward(plan, own, swap(other, "col"), table)
        total = (keep.astype(jnp.float32) + swap(send, "ta").astype(jnp.float32)).astype(jnp.bfloat16)
        return [total[0]] + [shift(total[k], k) for k in range(1, plan.gz)]

    def collect(pieces):
        keep, send = depth_forward(plan, pieces, zf)
        return keep, swap(send, "ta")

    def inward(keep, send, table):
        pieces = depth_inverse(plan, keep, swap(send, "ta"), zi, chunks)
        out = []
        for chunk in pieces:
            mine = jnp.stack([chunk[0]] + [shift(chunk[k], -k) for k in range(1, plan.gz)])
            own = time_inverse(plan, mine, swap(mine, "ta"), table)
            out.append((own, swap(own, "col")))
        return out

    t_fwd, t_inv = (pick(t, ta_at) for t in plain)
    tw_fwd, tw_inv = (pick(t, ta_at) for t in weighted)

    pieces = []
    for n in range(chunks):
        own, other = analyse_xy(plan, tiles, field, ty, n * zc, zc)
        pieces.append(outward(own, other, t_fwd))
    spec = collect(pieces)
    mixed = mix_modes(plan, spec, weights, here, perm, unit)
    planes = inward(*mixed, tw_inv)
    pieces, gprime = [], []
    for n in range(chunks):
        g, own, other = field_pass(
            plan, tiles, windows, *planes[n], field, mix_out, ty, ty_inv, xi, n * zc, zc,
            cot=cotangent, bias=point_bias,
        )
        gprime.append(g)
        pieces.append(outward(own, other, tw_fwd))
    grad = collect(pieces)
    back = back_modes(plan, grad, weights, here, perm)
    planes = inward(*back, t_inv)
    weight_grad = weight_modes(plan, spec, grad, here, perm, unit)
    full = None
    for n in range(chunks):
        full = field_pass(
            plan, tiles, windows, *planes[n], gprime[n], mix_in, ty, ty_inv, xi, n * zc, zc, full=full
        )
    input_grad = full.reshape(plan.depth, plan.steps, WIDTH, plan.rows, LX)
    weight_grad = weight_grad.reshape(plan.kz, MT, WIDTH, WIDTH, 2, plan.owned)
    return input_grad, jnp.transpose(weight_grad, (0, 1, 5, 4, 2, 3))


def per_device(mesh, field, cotangent, spectral_weight, point_weight, point_bias):
    args = (field, cotangent, spectral_weight, point_weight, point_bias)
    depth, steps, _, rows, _ = field.shape
    plan = Plan(mesh, depth, steps, rows)
    fits = (
        plan.col == 2
        and plan.ta == 2
        and plan.owned % MX == 0
        and plan.owned % GROUP == 0
        and steps % 4 == 0
        and rows == 32
        and plan.kt * WIDTH <= LANE
        and depth % CHUNKS == 0
    )
    if fits:
        return direct_device(plan, *args)
    return general_device(*args)


def solution(mesh):
    placed = (
        P(("groups", "gz"), "ta", None, "col", None),
        P(("groups", "gz"), "ta", None, "col", None),
        P("ta", None, ("gz", "col"), None, None, None),
        P(),
        P(),
    )
    return jax.shard_map(
        functools.partial(per_device, mesh),
        mesh=mesh,
        in_specs=placed,
        out_specs=(
            P(("groups", "gz"), "ta", None, "col", None),
            P(("groups", "ta"), None, ("gz", "col"), None, None, None),
        ),
        check_vma=False,
    )
```

```python
import functools
import math

import jax
import jax.numpy as jnp
import ml_dtypes
import numpy as np
from jax import lax
from jax.experimental import pallas as pl
from jax.experimental.pallas import tpu as pltpu
from jax.sharding import PartitionSpec as P

LX = 128
LY = 64
LZ = 32
LT = 24
WIDTH = 20
MX = 24
MY = 24
MZ = 16
MT = 12
PAIRS = 576
LANE = 128
GROUP = 8
CHUNKS = 2
SHIFTS = True
PARTS = 1
UNROLL = 4
COST = 0.1
WEIGHT_SIZES = (8,)
WHOLE = True
ORDERED = False


def wave_parts(length, mode_count, halfband):
    mode_index = jnp.arange(mode_count, dtype=jnp.int32)
    if halfband:
        frequency = mode_index
    else:
        frequency = jnp.where(mode_index < mode_count // 2, mode_index, mode_index - mode_count)
    places = jnp.arange(length, dtype=jnp.int32)
    phase_turns = places[:, None] * frequency[None, :] % length
    angles = phase_turns.astype(jnp.float32) * (2.0 * math.pi / length)
    scaling = 1.0 / math.sqrt(length)
    return (jnp.cos(angles) * scaling, jnp.sin(angles) * scaling)


def complex_table(length, mode_count, halfband, doubled, inverse):
    cosine, sine_part = wave_parts(length, mode_count, halfband)
    if doubled:
        factor = jnp.where(jnp.arange(mode_count) == 0, 1.0, 2.0).astype(jnp.float32)
        cosine = cosine * factor[None, :]
        sine_part = sine_part * factor[None, :]
    if inverse:
        table_out = jnp.stack(
            [jnp.stack([cosine, sine_part], -1), jnp.stack([-sine_part, cosine], -1)], 2
        )
        return jnp.transpose(table_out, (1, 0, 2, 3)).astype(jnp.bfloat16)
    table_out = jnp.stack(
        [jnp.stack([cosine, -sine_part], -1), jnp.stack([sine_part, cosine], -1)], 2
    )
    return table_out.astype(jnp.bfloat16)


def real_tables(length, mode_count):
    cosine, sine_part = wave_parts(length, mode_count, False)
    forward = jnp.stack([cosine, -sine_part], 0).astype(jnp.bfloat16)
    x_forward = jnp.transpose(forward, (1, 0, 2)).reshape(length, 2 * mode_count)
    x_inverse = jnp.transpose(forward, (0, 2, 1)).reshape(2 * mode_count, length)
    return (x_forward, x_inverse)


def product(pattern, first_op, second_op):
    return jnp.einsum(pattern, first_op, second_op, preferred_element_type=jnp.float32)


def gelu_slope(values):
    normal_cdf = 0.5 * (1.0 + lax.erf(values / math.sqrt(2.0)))
    return normal_cdf + values * jnp.exp(-0.5 * values * values) / math.sqrt(2.0 * math.pi)


def general_device(field, cotangent, spectral_weight, point_weight, point_bias):
    col_index = lax.axis_index("col")
    gz_count = lax.axis_size("gz")
    col_count = lax.axis_size("col")
    depth = field.shape[0]
    steps_here = field.shape[1]
    row_count = field.shape[3]
    owners = gz_count * col_count
    owned_pairs = PAIRS // owners
    x_fwd, x_inv = real_tables(LX, MX)
    y_fwd = lax.dynamic_slice_in_dim(
        complex_table(LY, MY, False, False, False), col_index * row_count, row_count, 0
    )
    y_inv = lax.dynamic_slice_in_dim(
        complex_table(LY, MY, False, False, True), col_index * row_count, row_count, 1
    )
    z_fwd = complex_table(LZ, MZ, False, False, False)
    z_inv = complex_table(LZ, MZ, False, False, True)
    t_plain_fwd = complex_table(LT, MT, True, False, False)
    t_weighted_fwd = complex_table(LT, MT, True, True, False)
    t_plain_inv = complex_table(LT, MT, True, False, True)
    t_weighted_inv = complex_table(LT, MT, True, True, True)

    def analyse(field_in, t_table):
        along_x = product("ztcyx,xj->ztcyj", field_in, x_fwd).astype(jnp.bfloat16)
        along_x = along_x.reshape(depth, steps_here, WIDTH, row_count, 2, MX)
        partial_sums = product("ztcyrk,ybrs->ztcsbk", along_x, y_fwd)
        spread = partial_sums.reshape(depth, steps_here, WIDTH, 2, gz_count, col_count, owned_pairs)
        halves = lax.psum_scatter(
            spread.astype(jnp.bfloat16), "col", scatter_dimension=5, tiled=True
        )
        mine = halves.reshape(depth, steps_here, WIDTH, 2, gz_count, owned_pairs)
        moved = lax.all_to_all(mine, "gz", split_axis=4, concat_axis=0, tiled=True)
        owned = moved.reshape(LZ, steps_here, WIDTH, 2, owned_pairs)
        along_z = product("ztcrm,zkrs->ktcsm", owned, z_fwd).astype(jnp.bfloat16)
        full_time = lax.all_to_all(along_z, "ta", split_axis=0, concat_axis=1, tiled=True)
        return product("ktcrm,tqrs->kqcsm", full_time, t_table).astype(jnp.bfloat16)

    def synthesize(spectrum_in, t_table):
        along_t = product("kqorm,qtrs->ktosm", spectrum_in, t_table).astype(jnp.bfloat16)
        own_steps = lax.all_to_all(along_t, "ta", split_axis=1, concat_axis=0, tiled=True)
        along_z = product("ktorm,kzrs->ztosm", own_steps, z_inv).astype(jnp.bfloat16)
        blocks = along_z.reshape(gz_count, depth, steps_here, WIDTH, 2, owned_pairs)
        copies = jnp.broadcast_to(
            blocks[:, None], (gz_count, col_count, depth, steps_here, WIDTH, 2, owned_pairs)
        )
        copies = copies.reshape(owners, depth, steps_here, WIDTH, 2, owned_pairs)
        gathered = lax.all_to_all(copies, ("gz", "col"), split_axis=0, concat_axis=5, tiled=True)
        split_pairs = gathered.reshape(depth, steps_here, WIDTH, 2, MY, MX)
        along_y = product("ztcrbk,byrs->ztcysk", split_pairs, y_inv).astype(jnp.bfloat16)
        along_y = along_y.reshape(depth, steps_here, WIDTH, row_count, 2 * MX)
        return product("ztcyj,jx->ztcyx", along_y, x_inv)

    spectrum = analyse(field, t_plain_fwd)
    real_in = spectrum[:, :, :, 0]
    imag_in = spectrum[:, :, :, 1]
    real_w = spectral_weight[:, :, :, 0]
    imag_w = spectral_weight[:, :, :, 1]
    mixed_real = product("kqim,kqmio->kqom", real_in, real_w) - product(
        "kqim,kqmio->kqom", imag_in, imag_w
    )
    mixed_imag = product("kqim,kqmio->kqom", real_in, imag_w) + product(
        "kqim,kqmio->kqom", imag_in, real_w
    )
    mixed = jnp.stack([mixed_real, mixed_imag], 3).astype(jnp.bfloat16)
    spectral = synthesize(mixed, t_weighted_inv)
    preact = (
        spectral
        + product("ztcyx,co->ztoyx", field, point_weight)
        + point_bias[None, None, :, None, None]
    )
    gprime = (cotangent.astype(jnp.float32) * gelu_slope(preact)).astype(jnp.bfloat16)
    gspec = analyse(gprime, t_weighted_fwd)
    grad_real = gspec[:, :, :, 0]
    grad_imag = gspec[:, :, :, 1]
    weight_real = product("kqim,kqom->kqmio", real_in, grad_real) + product(
        "kqim,kqom->kqmio", imag_in, grad_imag
    )
    weight_imag = product("kqim,kqom->kqmio", real_in, grad_imag) - product(
        "kqim,kqom->kqmio", imag_in, grad_real
    )
    weight_grad = jnp.stack([weight_real, weight_imag], 3).astype(jnp.bfloat16)
    back_real = product("kqom,kqmio->kqim", grad_real, real_w) + product(
        "kqom,kqmio->kqim", grad_imag, imag_w
    )
    back_imag = product("kqom,kqmio->kqim", grad_imag, real_w) - product(
        "kqom,kqmio->kqim", grad_real, imag_w
    )
    dspec = jnp.stack([back_real, back_imag], 3).astype(jnp.bfloat16)
    back_field = synthesize(dspec, t_plain_inv)
    input_grad = (back_field + product("ztoyx,co->ztcyx", gprime, point_weight)).astype(
        jnp.bfloat16
    )
    return (input_grad, weight_grad)


def waves(length, frequencies, places):
    turns = (np.asarray(places)[:, None] * np.asarray(frequencies)[None, :]) % length
    angles = turns * (2.0 * math.pi / length)
    scaling = 1.0 / math.sqrt(length)
    return np.cos(angles) * scaling, np.sin(angles) * scaling


def signed(count):
    return [k if k < count // 2 else k - count for k in range(count)]


def bf16(table):
    return np.asarray(table, dtype=np.float32).astype(ml_dtypes.bfloat16)


def place(own, k, count):
    return (own + k) % count if SHIFTS else abs(k)


class Plan:
    def __init__(self, mesh, depth, steps, rows):
        self.gz, self.ta, self.col = mesh.shape["gz"], mesh.shape["ta"], mesh.shape["col"]
        self.depth, self.steps, self.rows = depth, steps, rows
        self.owned = PAIRS // (self.gz * self.col)
        self.ky_own = self.owned // MX
        self.ky_half = MY // self.col
        self.lanes = self.ky_half * 2 * MX
        self.wide = (self.lanes + LANE - 1) // LANE * LANE
        self.half_pairs = self.ky_half * MX
        self.kt = MT // self.ta
        self.kz = MZ // self.ta
        self.grid_rows = steps * WIDTH

    def y_tables(self):
        out = np.zeros((self.gz, self.col, 2 * MY * GROUP, GROUP * self.rows), np.float32)
        freq = np.array(signed(MY))
        for a in range(self.gz):
            for b in range(self.col):
                order = [
                    self.ky_own * (self.col * place(a, k, self.gz) + (b ^ h)) + j
                    for h in range(self.col)
                    for k in range(self.gz)
                    for j in range(self.ky_own)
                ]
                places = np.arange(self.rows) + b * self.rows
                c, s = waves(LY, freq[order], places)
                part = np.stack([c.T, -s.T], 0)
                full = np.einsum("sky,gh->skghy", part, np.eye(GROUP))
                out[a, b] = full.reshape(out.shape[2:])
        return bf16(out.reshape(self.gz * self.col, *out.shape[2:]))

    def x_tiles(self):
        c, s = waves(LX, signed(MX), np.arange(LX))
        one = np.zeros((2, LX, 2, MX))
        one[0, :, 0], one[1, :, 0], one[0, :, 1], one[1, :, 1] = c, s, -s, c
        one = one.reshape(2 * LX, 2 * MX)
        tiles = []
        for low in range(0, self.lanes, 256):
            high = min(low + 256, self.lanes)
            kys = [k for k in range(self.ky_half) if k * 2 * MX < high and (k + 1) * 2 * MX > low]
            table = np.zeros((len(kys), 2 * LX, self.lanes), np.float32)
            for n, k in enumerate(kys):
                table[n, :, k * 2 * MX : (k + 1) * 2 * MX] = one
            table = table[:, :, low:high].reshape(len(kys) * 2 * LX, high - low)
            tiles.append((low, high, kys, bf16(table)))
        return tiles

    def x_windows(self):
        c, s = waves(LX, signed(MX), np.arange(LX))
        one = np.zeros((2, MX, 2, LX))
        one[0, :, 0], one[1, :, 0], one[0, :, 1], one[1, :, 1] = c.T, -s.T, s.T, c.T
        one = one.reshape(2 * MX, 2 * LX)
        windows, table = [], np.zeros((self.ky_half, 256, 2 * LX), np.float32)
        for k in range(self.ky_half):
            low = k * 2 * MX // 128 * 128
            high = min(low + 256, self.lanes)
            table[k, k * 2 * MX - low : (k + 1) * 2 * MX - low] = one
            windows.append((low, high))
        return windows, bf16(table)

    def t_tables(self, weighted):
        weight = np.array([1.0] + [2.0] * (MT - 1)) if weighted else np.ones(MT)
        gp = self.grid_rows_padded()
        eye = np.eye(WIDTH)
        fwd = np.zeros((self.ta, self.grid_rows, 2, self.ta, LANE), np.float32)
        inv = np.zeros((self.ta, self.ta, 2, LANE, 2, gp), np.float32)
        for a in range(self.ta):
            c, s = waves(LT, np.arange(MT), np.arange(self.steps) + a * self.steps)
            c, s = bf16(c * weight).astype(np.float32), bf16(s * weight).astype(np.float32)
            for h in range(self.ta):
                pick = slice((a ^ h) * self.kt, ((a ^ h) + 1) * self.kt)
                n = self.kt * WIDTH
                kc = np.einsum("tk,cd->tckd", c[:, pick], eye).reshape(self.grid_rows, n)
                ks = np.einsum("tk,cd->tckd", s[:, pick], eye).reshape(self.grid_rows, n)
                fwd[a, :, 0, h, :n], fwd[a, :, 1, h, :n] = kc, -ks
                g = self.grid_rows
                inv[a, h, 0, :n, 0, :g], inv[a, h, 1, :n, 0, :g] = kc.T, -ks.T
                inv[a, h, 0, :n, 1, :g], inv[a, h, 1, :n, 1, :g] = ks.T, kc.T
        fwd = fwd.reshape(self.ta, self.grid_rows, 2 * self.ta * LANE)
        return bf16(fwd), bf16(inv.reshape(self.ta, self.ta * 2 * LANE, 2 * gp))

    def grid_rows_padded(self):
        return (self.grid_rows + LANE - 1) // LANE * LANE

    def z_tables(self):
        shape = (self.ta, 2, self.kz, 2, self.gz, self.depth)
        fwd = np.zeros((self.gz, self.ta) + shape, np.float32)
        inv = np.zeros_like(fwd)
        freq = np.array(signed(MZ))
        for a in range(self.gz):
            places = np.concatenate(
                [np.arange(self.depth) + place(a, -k, self.gz) * self.depth for k in range(self.gz)]
            )
            for b in range(self.ta):
                for h in range(self.ta):
                    own = freq[(b ^ h) * self.kz : ((b ^ h) + 1) * self.kz]
                    c, s = waves(LZ, own, places)
                    c, s = (v.T.reshape(self.kz, self.gz, self.depth) for v in (c, s))
                    f, i = fwd[a, b, h], inv[a, b, h]
                    f[0, :, 0], f[0, :, 1], f[1, :, 0], f[1, :, 1] = c, s, -s, c
                    i[0, :, 0], i[0, :, 1], i[1, :, 0], i[1, :, 1] = c, s, -s, c
        eye = np.eye(GROUP)
        n = self.gz * self.ta
        f = np.einsum("abhskrmz,pq->abhskprmzq", fwd, eye)
        i = np.einsum("abhskrmz,pq->abrmzphskq", inv, eye)
        rows = self.ta * 2 * self.kz * GROUP
        cols = 2 * self.gz * self.depth * GROUP
        return bf16(f.reshape(n, rows, cols)), bf16(i.reshape(n, cols, rows))

    def pair_rows(self):
        n = self.kt * WIDTH
        table = np.zeros((self.ta, n, 2, self.ta, 2, LANE), np.float32)
        for h in range(self.ta):
            for r in range(2):
                table[h, np.arange(n), r, h, r, np.arange(n)] = 1.0
        return bf16(table.reshape(self.ta * n * 2, self.ta * 2 * LANE))


def dot(a, b):
    return jnp.dot(a, b, preferred_element_type=jnp.float32)


def dot_nt(a, b):
    return lax.dot_general(a, b, (((1,), (1,)), ((), ())), preferred_element_type=jnp.float32)


def slope_of(v):
    e = jnp.exp(-0.5 * v * v)
    d = 1.0 + (0.3275911 / math.sqrt(2.0)) * jnp.abs(v)
    t = pl.reciprocal(d, approx=True)
    t = t * (2.0 - d * t)
    poly = t * (
        0.5 * 0.254829592
        + t
        * (
            0.5 * -0.284496736
            + t * (0.5 * 1.421413741 + t * (0.5 * -1.453152027 + t * (0.5 * 1.061405429)))
        )
    )
    tail = poly * e
    cdf = jnp.where(v >= 0.0, 1.0 - tail, tail)
    return cdf + v * e * (1.0 / math.sqrt(2.0 * math.pi))


def whole_block(a):
    return pl.BlockSpec(a.shape, lambda *i, n=a.ndim: (0,) * n)


def spread_y(plan, fields, base, count, ty, us):
    for q in range(count // (2 * GROUP)):
        g = pl.multiple_of(base + q * 2 * GROUP, 2 * GROUP)
        a = fields[0, pl.ds(g, GROUP)].reshape(GROUP * plan.rows, LX)
        b = fields[0, pl.ds(g + GROUP, GROUP)].reshape(GROUP * plan.rows, LX)
        u = dot(ty, jnp.concatenate([a, b], 1))
        ua = u[:, :LX].reshape(2 * MY, GROUP, LX)
        ub = u[:, LX:].reshape(2 * MY, GROUP, LX)
        us[:, pl.ds(g, 2 * GROUP), :] = jnp.concatenate([ua, ub], 1).astype(jnp.bfloat16)


def gather_x(plan, tiles, us, tables, outs):
    for h in range(plan.col):
        for (low, high, kys, _), table in zip(tiles, tables):
            parts = []
            for k in kys:
                ky = h * plan.ky_half + k
                parts += [us[ky], us[MY + ky]]
            o = dot(jnp.concatenate(parts, 1), table[...])
            outs[h][0, :, low:high] = o.astype(jnp.bfloat16)


def rows_call(kernel, n, ids, grid, inputs, specs, out_shapes, out_specs, scratch, us, after=(), aliases=None, vmem=24):
    count, skip = len(inputs), len(after)
    any_spec = pl.BlockSpec(memory_space=pl.ANY)

    def body(ids_ref, *refs):
        kernel(ids_ref, *refs[:count], *refs[count + skip :])

    return pl.pallas_call(
        body,
        grid_spec=pltpu.PrefetchScalarGridSpec(
            num_scalar_prefetch=1,
            grid=(grid,),
            in_specs=list(specs) + [any_spec] * skip,
            out_specs=out_specs,
            scratch_shapes=scratch,
        ),
        out_shape=out_shapes,
        input_output_aliases=aliases or {},
        compiler_params=pltpu.CompilerParams(vmem_limit_bytes=vmem << 20),
        name=n,
        cost_estimate=pl.CostEstimate(
            flops=int(us * COST * 1.1e9), bytes_accessed=int(us * COST * 1e6), transcendentals=0
        ),
    )(ids, *inputs, *after)


def pick_block(a, which):
    return pl.BlockSpec((None,) + a.shape[1:], lambda z, ids, n=a.ndim: (ids[which],) + (0,) * (n - 1))


def repeat_rows(m, count):
    n, bits = WIDTH * count, count.bit_length() - 1
    iota = lambda shape, axis: lax.broadcasted_iota(jnp.int32, shape, axis)
    up = lax.shift_right_logical(iota((n, WIDTH), 0), bits) == iota((n, WIDTH), 1)
    up = up.astype(jnp.float32).astype(jnp.bfloat16)
    full = dot_nt(dot(up, m).astype(jnp.bfloat16), up)
    same = ((iota((n, n), 0) ^ iota((n, n), 1)) & (count - 1)) == 0
    return jnp.where(same, full, 0.0).astype(jnp.bfloat16)


def analyse_xy(plan, ids, tiles, field, ty, z0, zc, at, count, after, prev):
    def kernel(ids_ref, f, ty_ref, *refs):
        tables, outs, us = refs[: len(tiles)], refs[len(tiles) : -1], refs[-1]
        step = 5 * 2 * GROUP

        def body(i, carry):
            spread_y(plan, f, i * step, step, ty_ref[...], us)
            return carry

        lax.fori_loop(0, plan.grid_rows // step, body, 0)
        gather_x(plan, tiles, us, tables, outs)

    tabs = [jnp.asarray(t[3]) for t in tiles]
    out = jax.ShapeDtypeStruct((zc, plan.grid_rows, plan.wide), jnp.bfloat16)
    block = pl.BlockSpec((1, plan.grid_rows, plan.wide), lambda z, ids: (at + z, 0, 0))
    fspec = pl.BlockSpec((1, plan.grid_rows, plan.rows, LX), lambda z, ids: (z0 + at + z, 0, 0, 0))
    aliases = {1 + 2 + len(tabs) + i: i for i in range(len(prev))}
    return rows_call(
        kernel, "analyse_xy", ids, count, [field, ty, *tabs],
        [fspec, pick_block(ty, 0)] + [whole_block(t) for t in tabs],
        [out, out], [block, block],
        [pltpu.VMEM((2 * MY, plan.grid_rows, LX), jnp.bfloat16)], 2.8 * count, [*prev, *after], aliases, 52,
    )


def field_pass(plan, ids, tiles, windows, own, other, field, point, ty, ty_inv, xi, z0, zc, at, count, after, prev, cot=None, bias=None):
    first = cot is not None
    tabs = [jnp.asarray(t[3]) for t in tiles] if first else []
    block_rows = 4 * WIDTH
    half = plan.rows // 2
    pair = 2 * GROUP
    at0 = at

    def kernel(ids_ref, *refs):
        refs = list(refs)
        s_refs = (refs.pop(0), refs.pop(0))
        f, point_ref, tyi, xi_ref = refs.pop(0), refs.pop(0), refs.pop(0), refs.pop(0)
        if first:
            c_ref, bias_ref, ty_ref = refs.pop(0), refs.pop(0), refs.pop(0)
            tables = [refs.pop(0) for _ in tabs]
            g_out = refs.pop(0)
            outs = (refs.pop(0), refs.pop(0))
            us = refs.pop()
        else:
            g_out = refs.pop(0)
        ws, pre, mix = refs

        @pl.when(pl.program_id(0) == 0)
        def _():
            mix[...] = repeat_rows(point_ref[...], half)

        z = at0 + pl.program_id(0) if WHOLE else 0
        for h in range(plan.col):
            for k in range(plan.ky_half):
                low, high = windows[k]
                w = dot(s_refs[h][z, :, low:high], xi_ref[k, : high - low])
                ws[h * plan.ky_half + k] = w[:, :LX]
                ws[MY + h * plan.ky_half + k] = w[:, LX:]

        def block(i, carry):
            base = pl.multiple_of(i * block_rows, block_rows)
            rhs = lambda g: ws[:, pl.ds(g, GROUP), :].reshape(2 * MY * GROUP, LX).astype(jnp.bfloat16)

            def pointwise(t):
                v = f[0, pl.ds(base + t * WIDTH, WIDTH)]
                a = v[:, :half].reshape(WIDTH * half, LX)
                b = v[:, half:].reshape(WIDTH * half, LX)
                o = dot(mix[...], jnp.concatenate([a, b], 1))
                at = t * WIDTH
                pre[at : at + WIDTH, :half] = o[:, :LX].reshape(WIDTH, half, LX)
                pre[at : at + WIDTH, half:] = o[:, LX:].reshape(WIDTH, half, LX)

            def inverse(q):
                g = pl.multiple_of(base + q * pair, GROUP)
                o = dot(tyi[...], jnp.concatenate([rhs(g), rhs(g + GROUP)], 1))
                return o[:, :LX].reshape(GROUP, plan.rows, LX), o[:, LX:].reshape(GROUP, plan.rows, LX)

            def finish(q, parts):
                for m in range(pair):
                    at = q * pair + m
                    v = pre[at] + parts[m // GROUP][m % GROUP]
                    if first:
                        c = c_ref[0, base + at].astype(jnp.float32)
                        v = c * slope_of(v + bias_ref[at % WIDTH])
                    g_out[0, base + at] = v.astype(jnp.bfloat16)

            count = block_rows // pair
            for t in range(block_rows // WIDTH):
                pointwise(t)
            parts = inverse(0)
            for q in range(count):
                following = inverse(q + 1) if q + 1 < count else None
                finish(q, parts)
                parts = following
                if first:
                    spread_y(plan, g_out, base + q * pair, pair, ty_ref[...], us)
            return carry

        lax.fori_loop(0, plan.grid_rows // block_rows, block, 0)
        if first:
            gather_x(plan, tiles, us, tables, outs)

    cell = (1, plan.grid_rows, plan.rows, LX)
    local = pl.BlockSpec(cell, lambda z, ids: (at + z, 0, 0, 0))
    placed = pl.BlockSpec(cell, lambda z, ids: (z0 + at + z, 0, 0, 0))
    sblock = pl.BlockSpec((1, plan.grid_rows, plan.wide), lambda z, ids: (at + z, 0, 0))
    scratch = [
        pltpu.VMEM((2 * MY, plan.grid_rows, LX), jnp.float32),
        pltpu.VMEM((block_rows, plan.rows, LX), jnp.float32),
        pltpu.VMEM((WIDTH * half, WIDTH * half), jnp.bfloat16),
    ]
    inputs = [own, other, field, point, ty_inv, xi]
    kept = whole_block(own) if WHOLE else sblock
    specs = [kept, kept, placed if first else local, whole_block(point), pick_block(ty_inv, 0), whole_block(xi)]
    if first:
        inputs += [cot, bias, ty, *tabs]
        specs += [placed, pl.BlockSpec(memory_space=pltpu.SMEM), pick_block(ty, 0)]
        specs += [whole_block(t) for t in tabs]
        spec = jax.ShapeDtypeStruct((zc, plan.grid_rows, plan.wide), jnp.bfloat16)
        gout = jax.ShapeDtypeStruct((zc,) + cell[1:], jnp.bfloat16)
        shapes, out_specs, us, name = [gout, spec, spec], [local, sblock, sblock], 9.6, "slope_pass"
        scratch.append(pltpu.VMEM((2 * MY, plan.grid_rows, LX), jnp.bfloat16))
    else:
        shapes, out_specs = [jax.ShapeDtypeStruct((plan.depth,) + cell[1:], jnp.bfloat16)], [placed]
        us, name = 4.4, "input_pass"
    aliases = {1 + len(inputs) + i: i for i in range(len(prev))}
    return rows_call(
        kernel, name, ids, count, inputs, specs, shapes, out_specs, scratch, us * count, [*prev, *after], aliases, 42
    )


def time_forward(plan, ids, own, other, table):
    zc = own.shape[0]

    def kernel(ids_ref, a_ref, b_ref, m_ref, keep, send):
        for z in range(zc):
            a = a_ref[z, :, : plan.lanes].astype(jnp.float32) + b_ref[z, :, : plan.lanes].astype(jnp.float32)
            at = jnp.transpose(a).astype(jnp.bfloat16)
            p = dot(at, m_ref[...]).reshape(plan.ky_half, 2, MX, 4 * LANE)
            re = p[:, 0, :, : 2 * LANE] - p[:, 1, :, 2 * LANE :]
            im = p[:, 0, :, 2 * LANE :] + p[:, 1, :, : 2 * LANE]
            re, im = (v.reshape(plan.gz, plan.owned, 2 * LANE).astype(jnp.bfloat16) for v in (re, im))
            keep[:, z, :, :LANE], keep[:, z, :, LANE:] = re[..., :LANE], im[..., :LANE]
            send[:, z, :, :LANE], send[:, z, :, LANE:] = re[..., LANE:], im[..., LANE:]

    out = jax.ShapeDtypeStruct((plan.gz, zc, plan.owned, 2 * LANE), jnp.bfloat16)
    return rows_call(
        kernel, "time_forward", ids, 1, [own, other, table],
        [whole_block(own), whole_block(other), pick_block(table, 2)], [out, out], [whole_block(out)] * 2, [], 0.4 * zc,
    )


def time_inverse(plan, ids, keep, got, table, after):
    zc = keep[0].shape[1]
    gp = plan.grid_rows_padded()
    flat = [*keep, *got]

    def kernel(ids_ref, *refs):
        ins, m_ref, out = refs[: len(flat)], refs[-2], refs[-1]
        for z in range(zc):
            stacked = lambda rs: jnp.concatenate([r[:, z].reshape(-1, 2 * LANE) for r in rs], 0)
            a, b = stacked(ins[: len(keep)]), stacked(ins[len(keep) :])
            o = dot(jnp.concatenate([a, b], 1), m_ref[...]).reshape(plan.ky_half, 1, MX, 2 * gp)
            o = jnp.concatenate([o[..., :gp], o[..., gp:]], 1).reshape(plan.lanes, gp)
            out[z, :, : plan.lanes] = jnp.transpose(o)[: plan.grid_rows].astype(jnp.bfloat16)

    out = jax.ShapeDtypeStruct((zc, plan.grid_rows, plan.wide), jnp.bfloat16)
    return rows_call(
        kernel, "time_inverse", ids, 1, [*flat, table],
        [whole_block(a) for a in flat] + [pick_block(table, 2)],
        [out], [whole_block(out)], [], 0.4 * zc, after,
    )[0]


def depth_forward(plan, ids, pieces, table):
    flat = [p for chunk in pieces for p in chunk]
    n = len(flat)
    zc = flat[0].shape[1]
    octets = plan.owned // GROUP
    count = plan.gz * plan.depth

    def kernel(ids_ref, *refs):
        ins, m_ref, keep, send, buf, out = refs[:n], refs[n], refs[n + 1], refs[n + 2], refs[n + 3], refs[n + 4]
        at = 0
        for ref in ins:
            for k in range(ref.shape[0]):
                c, shift = at // plan.gz, at % plan.gz
                first = shift * plan.depth + c * zc
                buf[first : first + zc] = ref[k].astype(jnp.float32)
                at += 1
        for o in range(octets):
            x = buf[:, o * GROUP : (o + 1) * GROUP, :].reshape(count * GROUP, 2 * LANE)
            x = jnp.concatenate([x[:, :LANE], x[:, LANE:]], 0).astype(jnp.bfloat16)
            y = dot(m_ref[...], x).reshape(plan.ta, 2, plan.kz, GROUP, LANE)
            for h in range(plan.ta):
                for s in range(2):
                    out[h, :, o * GROUP : (o + 1) * GROUP, s * LANE : (s + 1) * LANE] = y[h, s]
        keep[...] = out[0].astype(jnp.bfloat16)
        send[...] = out[1].astype(jnp.bfloat16)

    shape = jax.ShapeDtypeStruct((plan.kz, plan.owned, 2 * LANE), jnp.bfloat16)
    return rows_call(
        kernel, "depth_forward", ids, 1, [*flat, table], [whole_block(a) for a in flat] + [pick_block(table, 1)],
        [shape, shape], [pl.BlockSpec(shape.shape, lambda *i: (0, 0, 0))] * 2,
        [
            pltpu.VMEM((count, plan.owned, 2 * LANE), jnp.float32),
            pltpu.VMEM((plan.ta, plan.kz, plan.owned, 2 * LANE), jnp.float32),
        ], 1.4,
    )


def depth_inverse(plan, ids, keep, got, table, chunks):
    octets = plan.owned // GROUP
    zc = plan.depth // chunks
    count = plan.gz * plan.depth
    cut = plan.gz if SHIFTS else 1

    def kernel(ids_ref, a_ref, b_ref, m_ref, *refs):
        outs, buf, out = refs[:-2], refs[-2], refs[-1]
        buf[0] = a_ref[...].astype(jnp.float32)
        buf[1] = b_ref[...].astype(jnp.float32)
        for o in range(octets):
            rows = slice(o * GROUP, (o + 1) * GROUP)
            x = [
                buf[h, :, rows, s * LANE : (s + 1) * LANE].reshape(plan.kz * GROUP, LANE)
                for h in range(plan.ta)
                for s in range(2)
            ]
            y = dot(m_ref[...], jnp.concatenate(x, 0).astype(jnp.bfloat16))
            y = y.reshape(2, count, GROUP, LANE)
            for s in range(2):
                out[:, rows, s * LANE : (s + 1) * LANE] = y[s]
        for c in range(chunks):
            for k in range(plan.gz):
                at = k * plan.depth + c * zc
                outs[c * cut + k % cut][k // cut] = out[at : at + zc].astype(jnp.bfloat16)

    shape = jax.ShapeDtypeStruct((plan.gz // cut, zc, plan.owned, 2 * LANE), jnp.bfloat16)
    n = chunks * cut
    flat = rows_call(
        kernel, "depth_inverse", ids, 1, [keep, got, table],
        [whole_block(keep), whole_block(got), pick_block(table, 1)],
        [shape] * n, [pl.BlockSpec(shape.shape, lambda *i: (0, 0, 0, 0))] * n,
        [
            pltpu.VMEM((plan.ta, plan.kz, plan.owned, 2 * LANE), jnp.float32),
            pltpu.VMEM((count, plan.owned, 2 * LANE), jnp.float32),
        ], 1.4,
    )
    return [flat[c * cut : (c + 1) * cut] for c in range(chunks)]


def swap_pairs(v):
    n = v.shape[0]
    even = lax.rem(lax.broadcasted_iota(jnp.int32, v.shape, 0), 2) == 0
    return jnp.where(even, -pltpu.roll(v, n - 1, 0), pltpu.roll(v, 1, 0))


def to_comm(plan, rows_ref, perm, keep, send):
    o = dot(jnp.transpose(rows_ref[...]).astype(jnp.bfloat16), perm[...]).astype(jnp.bfloat16)
    keep[0] = o[:, : 2 * LANE]
    send[0] = o[:, 2 * LANE :]


def mode_specs(plan):
    mode_rows = MT * WIDTH * WIDTH * 2
    half = pl.BlockSpec((1, plan.owned, 2 * LANE), lambda k, ids: (k, 0, 0))
    weights = pl.BlockSpec((1, mode_rows, plan.owned), lambda k, ids: (k, 0, 0))
    return half, weights, mode_rows


def mix_modes(plan, ids, spec, weights, perm, unit):
    half, wspec, mode_rows = mode_specs(plan)
    per_t = WIDTH * WIDTH * 2
    wide = 2 * WIDTH

    def kernel(ids_ref, a_ref, b_ref, w_ref, perm_ref, unit_ref, keep, send, xs, ms):
        x = jnp.concatenate([a_ref[0], b_ref[0]], 1)
        xs[...] = dot_nt(unit_ref[...], x)

        def step(q, carry):
            h = q // plan.kt
            kt = q - h * plan.kt
            at = lax.rem(q + ids_ref[2] * plan.kt, MT)
            row = h * 2 * LANE + kt * WIDTH
            s1 = jnp.zeros((wide, plan.owned), jnp.float32)
            s2 = jnp.zeros((wide, plan.owned), jnp.float32)
            for i in range(0, WIDTH, 2):
                w = w_ref[0, pl.ds(pl.multiple_of(at * per_t + i * wide, 2 * wide), 2 * wide), :].astype(jnp.float32)
                for j in range(2):
                    wi = w[j * wide : (j + 1) * wide]
                    s1 += xs[pl.ds(row + i + j, 1), :] * wi
                    s2 += xs[pl.ds(row + LANE + i + j, 1), :] * wi
            ms[pl.ds(pl.multiple_of(q * wide, 8), wide), :] = s1 + swap_pairs(s2)
            return carry

        lax.fori_loop(0, MT, step, 0, unroll=UNROLL)
        to_comm(plan, ms, perm_ref, keep, send)

    shape = jax.ShapeDtypeStruct((plan.kz, plan.owned, 2 * LANE), jnp.bfloat16)
    return rows_call(
        kernel, "mix_modes", ids, plan.kz, [*spec, weights, perm, unit],
        [half, half, wspec, whole_block(perm), whole_block(unit)],
        [shape, shape], [half, half],
        [
            pltpu.VMEM((2 * plan.ta * LANE, plan.owned), jnp.float32),
            pltpu.VMEM((MT * wide, plan.owned), jnp.float32),
        ], 17.0, vmem=46,
    )


def back_modes(plan, ids, grad, weights, perm):
    half, wspec, mode_rows = mode_specs(plan)
    per_t = WIDTH * WIDTH * 2
    wide = 2 * WIDTH

    def kernel(ids_ref, a_ref, b_ref, w_ref, perm_ref, keep, send, gs, ms):
        gs[...] = dot_nt(perm_ref[...], jnp.concatenate([a_ref[0], b_ref[0]], 1))

        def step(q, carry):
            at = lax.rem(q + ids_ref[2] * plan.kt, MT)
            g = gs[pl.ds(pl.multiple_of(q * wide, 8), wide), :]
            g2 = -swap_pairs(g)
            rows = []
            for i in range(0, WIDTH, 2):
                w = w_ref[0, pl.ds(pl.multiple_of(at * per_t + i * wide, 2 * wide), 2 * wide), :].astype(jnp.float32)
                for j in range(2):
                    wi = w[j * wide : (j + 1) * wide]
                    rows.append(jnp.sum(g * wi, 0, keepdims=True))
                    rows.append(jnp.sum(g2 * wi, 0, keepdims=True))
            ms[pl.ds(pl.multiple_of(q * wide, 8), wide), :] = jnp.concatenate(rows, 0)
            return carry

        lax.fori_loop(0, MT, step, 0, unroll=UNROLL)
        to_comm(plan, ms, perm_ref, keep, send)

    shape = jax.ShapeDtypeStruct((plan.kz, plan.owned, 2 * LANE), jnp.bfloat16)
    return rows_call(
        kernel, "back_modes", ids, plan.kz, [*grad, weights, perm],
        [half, half, wspec, whole_block(perm)],
        [shape, shape], [half, half],
        [pltpu.VMEM((MT * wide, plan.owned), jnp.float32)] * 2, 20.0, vmem=46,
    )


def weight_modes(plan, ids, spec, grad, perm, unit, k0, count, full, after):
    _, _, mode_rows = mode_specs(plan)
    half = pl.BlockSpec((1, plan.owned, 2 * LANE), lambda k, ids: (k0 + k, 0, 0))
    wspec = pl.BlockSpec((1, mode_rows, plan.owned), lambda k, ids: (k0 + k, 0, 0))
    per_t = WIDTH * WIDTH * 2
    wide = 2 * WIDTH

    def kernel(ids_ref, xa, xb, ga, gb, perm_ref, unit_ref, out, xs, gs):
        xs[...] = dot_nt(unit_ref[...], jnp.concatenate([xa[0], xb[0]], 1))
        gs[...] = dot_nt(perm_ref[...], jnp.concatenate([ga[0], gb[0]], 1))

        def step(q, carry):
            h = q // plan.kt
            kt = q - h * plan.kt
            at = lax.rem(q + ids_ref[2] * plan.kt, MT)
            row = h * 2 * LANE + kt * WIDTH
            g = gs[pl.ds(pl.multiple_of(q * wide, 8), wide), :]
            g2 = -swap_pairs(g)
            for i in range(0, WIDTH, 2):
                two = [
                    xs[pl.ds(row + i + j, 1), :] * g + xs[pl.ds(row + LANE + i + j, 1), :] * g2
                    for j in range(2)
                ]
                rows = pl.ds(pl.multiple_of(at * per_t + i * wide, 2 * wide), 2 * wide)
                out[0, rows, :] = jnp.concatenate(two, 0).astype(jnp.bfloat16)
            return carry

        lax.fori_loop(0, MT, step, 0, unroll=UNROLL)

    shape = jax.ShapeDtypeStruct((plan.kz, mode_rows, plan.owned), jnp.bfloat16)
    return rows_call(
        kernel, "weight_modes", ids, count, [*spec, *grad, perm, unit],
        [half, half, half, half, whole_block(perm), whole_block(unit)],
        [shape], [wspec],
        [
            pltpu.VMEM((2 * plan.ta * LANE, plan.owned), jnp.float32),
            pltpu.VMEM((MT * wide, plan.owned), jnp.float32),
        ], 1.8 * count, [*([] if full is None else [full]), *after], {} if full is None else {7: 0}, 46,
    )[0]


def direct_device(plan, field, cotangent, spectral_weight, point_weight, point_bias):
    gz_at, ta_at, col_at = (lax.axis_index(a) for a in ("gz", "ta", "col"))
    chunks = CHUNKS
    zc = plan.depth // chunks
    ids = jnp.stack([gz_at * plan.col + col_at, gz_at * plan.ta + ta_at, ta_at]).astype(jnp.int32)
    y_table = plan.y_tables()
    ty, ty_inv = jnp.asarray(y_table), jnp.asarray(np.swapaxes(y_table, 1, 2).copy())
    tiles = plan.x_tiles()
    windows, xi = plan.x_windows()
    xi = jnp.asarray(xi)
    zf, zi = (jnp.asarray(t) for t in plan.z_tables())
    t_fwd, t_inv = (jnp.asarray(t) for t in plan.t_tables(False))
    tw_fwd, tw_inv = (jnp.asarray(t) for t in plan.t_tables(True))
    perm = jnp.asarray(plan.pair_rows())
    unit = jnp.asarray(bf16(np.eye(2 * plan.ta * LANE)))
    flat = (plan.depth, plan.grid_rows, plan.rows, LX)
    field, cotangent = field.reshape(flat), cotangent.reshape(flat)
    weights = jnp.transpose(spectral_weight, (0, 1, 4, 5, 3, 2))
    weights = weights.reshape(plan.kz, MT * WIDTH * WIDTH * 2, plan.owned)

    def swap(a, axis):
        return lax.ppermute(a, axis, [(0, 1), (1, 0)])

    def spread(blocks, sign):
        if not SHIFTS:
            return [lax.all_to_all(blocks[0], "gz", 0, 0, tiled=True)]
        moved = [blocks[0]]
        for k in range(1, plan.gz):
            moved.append(lax.ppermute(blocks[k], "gz", [(d, (d + sign * k) % plan.gz) for d in range(plan.gz)]))
        return moved

    def outward(own, other, table):
        keep, send = time_forward(plan, ids, own, swap(other, "col"), table)
        total = (keep.astype(jnp.float32) + swap(send, "ta").astype(jnp.float32)).astype(jnp.bfloat16)
        blocks = [total[k : k + 1] for k in range(plan.gz)] if SHIFTS else [total]
        return spread(blocks, 1), send

    def collect(pieces):
        keep, send = depth_forward(plan, ids, pieces, zf)
        return keep, swap(send, "ta")

    def inward(keep, send):
        out = []
        for chunk in depth_inverse(plan, ids, keep, swap(send, "ta"), zi, chunks):
            mine = spread(chunk, -1)
            if len(mine) > 1:
                mine = [jnp.concatenate(mine, 0)]
            out.append((mine, [swap(m, "ta") for m in mine]))
        return out

    def planes(pieces, table, after):
        own = time_inverse(plan, ids, *pieces, table, after)
        return own, swap(own, "col")

    sub = zc // PARTS
    pieces, sent = [], []
    for n in range(chunks):
        made = []
        for m in range(PARTS):
            after = [sent[n - 1]] if n and m == 1 else []
            made = analyse_xy(plan, ids, tiles, field, ty, n * zc, zc, m * sub, sub, after, made)
        moved, send = outward(*made, t_fwd)
        pieces.append(moved)
        sent.append(send)
    spec = collect(pieces)
    mixed = mix_modes(plan, ids, spec, weights, perm, unit)
    arrived = inward(*mixed)
    pieces, gprime, sent = [], [], []
    for n in range(chunks):
        made = []
        plane = planes(arrived[n], tw_inv, gprime[-1:] if n and ORDERED else [])
        for m in range(PARTS):
            after = [sent[n - 1]] if n and m == 1 else []
            made = field_pass(
                plan, ids, tiles, windows, *plane, field, point_weight.T, ty, ty_inv, xi,
                n * zc, zc, m * sub, sub, after, made, cot=cotangent, bias=point_bias,
            )
        g, own, other = made
        gprime.append(g)
        moved, send = outward(own, other, tw_fwd)
        pieces.append(moved)
        sent.append(send)
    grad = collect(pieces)
    back = back_modes(plan, ids, grad, weights, perm)
    arrived = inward(*back)
    weight_grad, at = None, 0
    for n, count in enumerate(WEIGHT_SIZES):
        after = arrived[0][0] if n == len(WEIGHT_SIZES) - 1 else []
        weight_grad = weight_modes(plan, ids, spec, grad, perm, unit, at, count, weight_grad, after)
        at += count
    made = []
    for n in range(chunks):
        plane = planes(arrived[n], t_inv, [weight_grad] if n == 0 else [])
        made = field_pass(
            plan, ids, tiles, windows, *plane, gprime[n], point_weight, ty, ty_inv, xi, n * zc, zc, 0, zc, [], made
        )
    input_grad = made[0].reshape(plan.depth, plan.steps, WIDTH, plan.rows, LX)
    weight_grad = weight_grad.reshape(plan.kz, MT, WIDTH, WIDTH, 2, plan.owned)
    return input_grad, jnp.transpose(weight_grad, (0, 1, 5, 4, 2, 3))


def per_device(mesh, field, cotangent, spectral_weight, point_weight, point_bias):
    args = (field, cotangent, spectral_weight, point_weight, point_bias)
    depth, steps, _, rows, _ = field.shape
    plan = Plan(mesh, depth, steps, rows)
    fits = (
        plan.col == 2
        and plan.ta == 2
        and plan.owned % MX == 0
        and plan.owned % GROUP == 0
        and steps % 4 == 0
        and rows == 32
        and plan.kt * WIDTH <= LANE
        and depth % CHUNKS == 0
        and plan.kz == sum(WEIGHT_SIZES)
    )
    if fits:
        return direct_device(plan, *args)
    return general_device(*args)


def solution(mesh):
    placed = (
        P(("groups", "gz"), "ta", None, "col", None),
        P(("groups", "gz"), "ta", None, "col", None),
        P("ta", None, ("gz", "col"), None, None, None),
        P(),
        P(),
    )
    return jax.shard_map(
        functools.partial(per_device, mesh),
        mesh=mesh,
        in_specs=placed,
        out_specs=(
            P(("groups", "gz"), "ta", None, "col", None),
            P(("groups", "ta"), None, ("gz", "col"), None, None, None),
        ),
        check_vma=False,
    )
```

```python
import functools
import math

import jax
import jax.numpy as jnp
import ml_dtypes
import numpy as np
from jax import lax
from jax.experimental import pallas as pl
from jax.experimental.pallas import tpu as pltpu
from jax.sharding import PartitionSpec as P

LX = 128
LY = 64
LZ = 32
LT = 24
WIDTH = 20
MX = 24
MY = 24
MZ = 16
MT = 12
PAIRS = 576
LANE = 128
GROUP = 8
CHUNKS = 2
SHIFTS = True
PARTS = 1
UNROLL = 4
COST = 0.1
WEIGHT_SIZES = (8,)
WHOLE = True
ORDERED = False
QUEUE_IN = True
QUEUE_OUT = False
EARLY = False
FAR = True
LAST_ORDERED = False


def wave_parts(length, mode_count, halfband):
    mode_index = jnp.arange(mode_count, dtype=jnp.int32)
    if halfband:
        frequency = mode_index
    else:
        frequency = jnp.where(mode_index < mode_count // 2, mode_index, mode_index - mode_count)
    places = jnp.arange(length, dtype=jnp.int32)
    phase_turns = places[:, None] * frequency[None, :] % length
    angles = phase_turns.astype(jnp.float32) * (2.0 * math.pi / length)
    scaling = 1.0 / math.sqrt(length)
    return (jnp.cos(angles) * scaling, jnp.sin(angles) * scaling)


def complex_table(length, mode_count, halfband, doubled, inverse):
    cosine, sine_part = wave_parts(length, mode_count, halfband)
    if doubled:
        factor = jnp.where(jnp.arange(mode_count) == 0, 1.0, 2.0).astype(jnp.float32)
        cosine = cosine * factor[None, :]
        sine_part = sine_part * factor[None, :]
    if inverse:
        table_out = jnp.stack(
            [jnp.stack([cosine, sine_part], -1), jnp.stack([-sine_part, cosine], -1)], 2
        )
        return jnp.transpose(table_out, (1, 0, 2, 3)).astype(jnp.bfloat16)
    table_out = jnp.stack(
        [jnp.stack([cosine, -sine_part], -1), jnp.stack([sine_part, cosine], -1)], 2
    )
    return table_out.astype(jnp.bfloat16)


def real_tables(length, mode_count):
    cosine, sine_part = wave_parts(length, mode_count, False)
    forward = jnp.stack([cosine, -sine_part], 0).astype(jnp.bfloat16)
    x_forward = jnp.transpose(forward, (1, 0, 2)).reshape(length, 2 * mode_count)
    x_inverse = jnp.transpose(forward, (0, 2, 1)).reshape(2 * mode_count, length)
    return (x_forward, x_inverse)


def product(pattern, first_op, second_op):
    return jnp.einsum(pattern, first_op, second_op, preferred_element_type=jnp.float32)


def gelu_slope(values):
    normal_cdf = 0.5 * (1.0 + lax.erf(values / math.sqrt(2.0)))
    return normal_cdf + values * jnp.exp(-0.5 * values * values) / math.sqrt(2.0 * math.pi)


def general_device(field, cotangent, spectral_weight, point_weight, point_bias):
    col_index = lax.axis_index("col")
    gz_count = lax.axis_size("gz")
    col_count = lax.axis_size("col")
    depth = field.shape[0]
    steps_here = field.shape[1]
    row_count = field.shape[3]
    owners = gz_count * col_count
    owned_pairs = PAIRS // owners
    x_fwd, x_inv = real_tables(LX, MX)
    y_fwd = lax.dynamic_slice_in_dim(
        complex_table(LY, MY, False, False, False), col_index * row_count, row_count, 0
    )
    y_inv = lax.dynamic_slice_in_dim(
        complex_table(LY, MY, False, False, True), col_index * row_count, row_count, 1
    )
    z_fwd = complex_table(LZ, MZ, False, False, False)
    z_inv = complex_table(LZ, MZ, False, False, True)
    t_plain_fwd = complex_table(LT, MT, True, False, False)
    t_weighted_fwd = complex_table(LT, MT, True, True, False)
    t_plain_inv = complex_table(LT, MT, True, False, True)
    t_weighted_inv = complex_table(LT, MT, True, True, True)

    def analyse(field_in, t_table):
        along_x = product("ztcyx,xj->ztcyj", field_in, x_fwd).astype(jnp.bfloat16)
        along_x = along_x.reshape(depth, steps_here, WIDTH, row_count, 2, MX)
        partial_sums = product("ztcyrk,ybrs->ztcsbk", along_x, y_fwd)
        spread = partial_sums.reshape(depth, steps_here, WIDTH, 2, gz_count, col_count, owned_pairs)
        halves = lax.psum_scatter(
            spread.astype(jnp.bfloat16), "col", scatter_dimension=5, tiled=True
        )
        mine = halves.reshape(depth, steps_here, WIDTH, 2, gz_count, owned_pairs)
        moved = lax.all_to_all(mine, "gz", split_axis=4, concat_axis=0, tiled=True)
        owned = moved.reshape(LZ, steps_here, WIDTH, 2, owned_pairs)
        along_z = product("ztcrm,zkrs->ktcsm", owned, z_fwd).astype(jnp.bfloat16)
        full_time = lax.all_to_all(along_z, "ta", split_axis=0, concat_axis=1, tiled=True)
        return product("ktcrm,tqrs->kqcsm", full_time, t_table).astype(jnp.bfloat16)

    def synthesize(spectrum_in, t_table):
        along_t = product("kqorm,qtrs->ktosm", spectrum_in, t_table).astype(jnp.bfloat16)
        own_steps = lax.all_to_all(along_t, "ta", split_axis=1, concat_axis=0, tiled=True)
        along_z = product("ktorm,kzrs->ztosm", own_steps, z_inv).astype(jnp.bfloat16)
        blocks = along_z.reshape(gz_count, depth, steps_here, WIDTH, 2, owned_pairs)
        copies = jnp.broadcast_to(
            blocks[:, None], (gz_count, col_count, depth, steps_here, WIDTH, 2, owned_pairs)
        )
        copies = copies.reshape(owners, depth, steps_here, WIDTH, 2, owned_pairs)
        gathered = lax.all_to_all(copies, ("gz", "col"), split_axis=0, concat_axis=5, tiled=True)
        split_pairs = gathered.reshape(depth, steps_here, WIDTH, 2, MY, MX)
        along_y = product("ztcrbk,byrs->ztcysk", split_pairs, y_inv).astype(jnp.bfloat16)
        along_y = along_y.reshape(depth, steps_here, WIDTH, row_count, 2 * MX)
        return product("ztcyj,jx->ztcyx", along_y, x_inv)

    spectrum = analyse(field, t_plain_fwd)
    real_in = spectrum[:, :, :, 0]
    imag_in = spectrum[:, :, :, 1]
    real_w = spectral_weight[:, :, :, 0]
    imag_w = spectral_weight[:, :, :, 1]
    mixed_real = product("kqim,kqmio->kqom", real_in, real_w) - product(
        "kqim,kqmio->kqom", imag_in, imag_w
    )
    mixed_imag = product("kqim,kqmio->kqom", real_in, imag_w) + product(
        "kqim,kqmio->kqom", imag_in, real_w
    )
    mixed = jnp.stack([mixed_real, mixed_imag], 3).astype(jnp.bfloat16)
    spectral = synthesize(mixed, t_weighted_inv)
    preact = (
        spectral
        + product("ztcyx,co->ztoyx", field, point_weight)
        + point_bias[None, None, :, None, None]
    )
    gprime = (cotangent.astype(jnp.float32) * gelu_slope(preact)).astype(jnp.bfloat16)
    gspec = analyse(gprime, t_weighted_fwd)
    grad_real = gspec[:, :, :, 0]
    grad_imag = gspec[:, :, :, 1]
    weight_real = product("kqim,kqom->kqmio", real_in, grad_real) + product(
        "kqim,kqom->kqmio", imag_in, grad_imag
    )
    weight_imag = product("kqim,kqom->kqmio", real_in, grad_imag) - product(
        "kqim,kqom->kqmio", imag_in, grad_real
    )
    weight_grad = jnp.stack([weight_real, weight_imag], 3).astype(jnp.bfloat16)
    back_real = product("kqom,kqmio->kqim", grad_real, real_w) + product(
        "kqom,kqmio->kqim", grad_imag, imag_w
    )
    back_imag = product("kqom,kqmio->kqim", grad_imag, real_w) - product(
        "kqom,kqmio->kqim", grad_real, imag_w
    )
    dspec = jnp.stack([back_real, back_imag], 3).astype(jnp.bfloat16)
    back_field = synthesize(dspec, t_plain_inv)
    input_grad = (back_field + product("ztoyx,co->ztcyx", gprime, point_weight)).astype(
        jnp.bfloat16
    )
    return (input_grad, weight_grad)


def waves(length, frequencies, places):
    turns = (np.asarray(places)[:, None] * np.asarray(frequencies)[None, :]) % length
    angles = turns * (2.0 * math.pi / length)
    scaling = 1.0 / math.sqrt(length)
    return np.cos(angles) * scaling, np.sin(angles) * scaling


def signed(count):
    return [k if k < count // 2 else k - count for k in range(count)]


def bf16(table):
    return np.asarray(table, dtype=np.float32).astype(ml_dtypes.bfloat16)


def place(own, k, count):
    return (own + k) % count if SHIFTS else abs(k)


class Plan:
    def __init__(self, mesh, depth, steps, rows):
        self.gz, self.ta, self.col = mesh.shape["gz"], mesh.shape["ta"], mesh.shape["col"]
        self.depth, self.steps, self.rows = depth, steps, rows
        self.owned = PAIRS // (self.gz * self.col)
        self.ky_own = self.owned // MX
        self.ky_half = MY // self.col
        self.lanes = self.ky_half * 2 * MX
        self.wide = (self.lanes + LANE - 1) // LANE * LANE
        self.half_pairs = self.ky_half * MX
        self.kt = MT // self.ta
        self.kz = MZ // self.ta
        self.grid_rows = steps * WIDTH

    def y_tables(self):
        out = np.zeros((self.gz, self.col, 2 * MY * GROUP, GROUP * self.rows), np.float32)
        freq = np.array(signed(MY))
        for a in range(self.gz):
            for b in range(self.col):
                order = [
                    self.ky_own * (self.col * place(a, k, self.gz) + (b ^ h)) + j
                    for h in range(self.col)
                    for k in range(self.gz)
                    for j in range(self.ky_own)
                ]
                places = np.arange(self.rows) + b * self.rows
                c, s = waves(LY, freq[order], places)
                part = np.stack([c.T, -s.T], 0)
                full = np.einsum("sky,gh->skghy", part, np.eye(GROUP))
                out[a, b] = full.reshape(out.shape[2:])
        return bf16(out.reshape(self.gz * self.col, *out.shape[2:]))

    def x_tiles(self):
        c, s = waves(LX, signed(MX), np.arange(LX))
        one = np.zeros((2, LX, 2, MX))
        one[0, :, 0], one[1, :, 0], one[0, :, 1], one[1, :, 1] = c, s, -s, c
        one = one.reshape(2 * LX, 2 * MX)
        tiles = []
        for low in range(0, self.lanes, 256):
            high = min(low + 256, self.lanes)
            kys = [k for k in range(self.ky_half) if k * 2 * MX < high and (k + 1) * 2 * MX > low]
            table = np.zeros((len(kys), 2 * LX, self.lanes), np.float32)
            for n, k in enumerate(kys):
                table[n, :, k * 2 * MX : (k + 1) * 2 * MX] = one
            table = table[:, :, low:high].reshape(len(kys) * 2 * LX, high - low)
            tiles.append((low, high, kys, bf16(table)))
        return tiles

    def x_windows(self):
        c, s = waves(LX, signed(MX), np.arange(LX))
        one = np.zeros((2, MX, 2, LX))
        one[0, :, 0], one[1, :, 0], one[0, :, 1], one[1, :, 1] = c.T, -s.T, s.T, c.T
        one = one.reshape(2 * MX, 2 * LX)
        windows, table = [], np.zeros((self.ky_half, 256, 2 * LX), np.float32)
        for k in range(self.ky_half):
            low = k * 2 * MX // 128 * 128
            high = min(low + 256, self.lanes)
            table[k, k * 2 * MX - low : (k + 1) * 2 * MX - low] = one
            windows.append((low, high))
        return windows, bf16(table)

    def t_tables(self, weighted):
        weight = np.array([1.0] + [2.0] * (MT - 1)) if weighted else np.ones(MT)
        gp = self.grid_rows_padded()
        eye = np.eye(WIDTH)
        fwd = np.zeros((self.ta, self.grid_rows, 2, self.ta, LANE), np.float32)
        inv = np.zeros((self.ta, self.ta, 2, LANE, 2, gp), np.float32)
        for a in range(self.ta):
            c, s = waves(LT, np.arange(MT), np.arange(self.steps) + a * self.steps)
            c, s = bf16(c * weight).astype(np.float32), bf16(s * weight).astype(np.float32)
            for h in range(self.ta):
                pick = slice((a ^ h) * self.kt, ((a ^ h) + 1) * self.kt)
                n = self.kt * WIDTH
                kc = np.einsum("tk,cd->tckd", c[:, pick], eye).reshape(self.grid_rows, n)
                ks = np.einsum("tk,cd->tckd", s[:, pick], eye).reshape(self.grid_rows, n)
                fwd[a, :, 0, h, :n], fwd[a, :, 1, h, :n] = kc, -ks
                g = self.grid_rows
                inv[a, h, 0, :n, 0, :g], inv[a, h, 1, :n, 0, :g] = kc.T, -ks.T
                inv[a, h, 0, :n, 1, :g], inv[a, h, 1, :n, 1, :g] = ks.T, kc.T
        fwd = fwd.reshape(self.ta, self.grid_rows, 2 * self.ta * LANE)
        return bf16(fwd), bf16(inv.reshape(self.ta, self.ta * 2 * LANE, 2 * gp))

    def grid_rows_padded(self):
        return (self.grid_rows + LANE - 1) // LANE * LANE

    def z_tables(self):
        shape = (self.ta, 2, self.kz, 2, self.gz, self.depth)
        fwd = np.zeros((self.gz, self.ta) + shape, np.float32)
        inv = np.zeros_like(fwd)
        freq = np.array(signed(MZ))
        for a in range(self.gz):
            places = np.concatenate(
                [np.arange(self.depth) + place(a, -k, self.gz) * self.depth for k in range(self.gz)]
            )
            for b in range(self.ta):
                for h in range(self.ta):
                    own = freq[(b ^ h) * self.kz : ((b ^ h) + 1) * self.kz]
                    c, s = waves(LZ, own, places)
                    c, s = (v.T.reshape(self.kz, self.gz, self.depth) for v in (c, s))
                    f, i = fwd[a, b, h], inv[a, b, h]
                    f[0, :, 0], f[0, :, 1], f[1, :, 0], f[1, :, 1] = c, s, -s, c
                    i[0, :, 0], i[0, :, 1], i[1, :, 0], i[1, :, 1] = c, s, -s, c
        eye = np.eye(GROUP)
        n = self.gz * self.ta
        f = np.einsum("abhskrmz,pq->abhskprmzq", fwd, eye)
        i = np.einsum("abhskrmz,pq->abrmzphskq", inv, eye)
        rows = self.ta * 2 * self.kz * GROUP
        cols = 2 * self.gz * self.depth * GROUP
        return bf16(f.reshape(n, rows, cols)), bf16(i.reshape(n, cols, rows))

    def pair_rows(self):
        n = self.kt * WIDTH
        table = np.zeros((self.ta, n, 2, self.ta, 2, LANE), np.float32)
        for h in range(self.ta):
            for r in range(2):
                table[h, np.arange(n), r, h, r, np.arange(n)] = 1.0
        return bf16(table.reshape(self.ta * n * 2, self.ta * 2 * LANE))


def dot(a, b):
    return jnp.dot(a, b, preferred_element_type=jnp.float32)


def dot_nt(a, b):
    return lax.dot_general(a, b, (((1,), (1,)), ((), ())), preferred_element_type=jnp.float32)


def slope_of(v):
    e = jnp.exp(-0.5 * v * v)
    d = 1.0 + (0.3275911 / math.sqrt(2.0)) * jnp.abs(v)
    t = pl.reciprocal(d, approx=True)
    t = t * (2.0 - d * t)
    poly = t * (
        0.5 * 0.254829592
        + t
        * (
            0.5 * -0.284496736
            + t * (0.5 * 1.421413741 + t * (0.5 * -1.453152027 + t * (0.5 * 1.061405429)))
        )
    )
    tail = poly * e
    cdf = jnp.where(v >= 0.0, 1.0 - tail, tail)
    return cdf + v * e * (1.0 / math.sqrt(2.0 * math.pi))


def whole_block(a):
    return pl.BlockSpec(a.shape, lambda *i, n=a.ndim: (0,) * n)


def spread_y(plan, fields, base, count, ty, us):
    for q in range(count // (2 * GROUP)):
        g = pl.multiple_of(base + q * 2 * GROUP, 2 * GROUP)
        a = fields[0, pl.ds(g, GROUP)].reshape(GROUP * plan.rows, LX)
        b = fields[0, pl.ds(g + GROUP, GROUP)].reshape(GROUP * plan.rows, LX)
        u = dot(ty, jnp.concatenate([a, b], 1))
        ua = u[:, :LX].reshape(2 * MY, GROUP, LX)
        ub = u[:, LX:].reshape(2 * MY, GROUP, LX)
        us[:, pl.ds(g, 2 * GROUP), :] = jnp.concatenate([ua, ub], 1).astype(jnp.bfloat16)


def gather_x(plan, tiles, us, tables, outs):
    for h in range(plan.col):
        for (low, high, kys, _), table in zip(tiles, tables):
            parts = []
            for k in kys:
                ky = h * plan.ky_half + k
                parts += [us[ky], us[MY + ky]]
            o = dot(jnp.concatenate(parts, 1), table[...])
            outs[h][0, :, low:high] = o.astype(jnp.bfloat16)


def rows_call(kernel, n, ids, grid, inputs, specs, out_shapes, out_specs, scratch, us, after=(), aliases=None, vmem=24):
    count, skip = len(inputs), len(after)
    any_spec = pl.BlockSpec(memory_space=pl.ANY)

    def body(ids_ref, *refs):
        kernel(ids_ref, *refs[:count], *refs[count + skip :])

    return pl.pallas_call(
        body,
        grid_spec=pltpu.PrefetchScalarGridSpec(
            num_scalar_prefetch=1,
            grid=(grid,),
            in_specs=list(specs) + [any_spec] * skip,
            out_specs=out_specs,
            scratch_shapes=scratch,
        ),
        out_shape=out_shapes,
        input_output_aliases=aliases or {},
        compiler_params=pltpu.CompilerParams(vmem_limit_bytes=vmem << 20),
        name=n,
        cost_estimate=pl.CostEstimate(
            flops=int(us * COST * 1.1e9), bytes_accessed=int(us * COST * 1e6), transcendentals=0
        ),
    )(ids, *inputs, *after)


def far(a):
    return pltpu.with_memory_space_constraint(a, pltpu.HBM) if FAR else a


def pick_block(a, which):
    return pl.BlockSpec((None,) + a.shape[1:], lambda z, ids, n=a.ndim: (ids[which],) + (0,) * (n - 1))


def repeat_rows(m, count):
    n, bits = WIDTH * count, count.bit_length() - 1
    iota = lambda shape, axis: lax.broadcasted_iota(jnp.int32, shape, axis)
    up = lax.shift_right_logical(iota((n, WIDTH), 0), bits) == iota((n, WIDTH), 1)
    up = up.astype(jnp.float32).astype(jnp.bfloat16)
    full = dot_nt(dot(up, m).astype(jnp.bfloat16), up)
    same = ((iota((n, n), 0) ^ iota((n, n), 1)) & (count - 1)) == 0
    return jnp.where(same, full, 0.0).astype(jnp.bfloat16)


def analyse_xy(plan, ids, tiles, field, ty, z0, zc, at, count, after, prev):
    def kernel(ids_ref, f, ty_ref, *refs):
        tables, outs, us = refs[: len(tiles)], refs[len(tiles) : -1], refs[-1]
        step = 5 * 2 * GROUP

        def body(i, carry):
            spread_y(plan, f, i * step, step, ty_ref[...], us)
            return carry

        lax.fori_loop(0, plan.grid_rows // step, body, 0)
        gather_x(plan, tiles, us, tables, outs)

    tabs = [far(jnp.asarray(t[3])) for t in tiles]
    out = jax.ShapeDtypeStruct((zc, plan.grid_rows, plan.wide), jnp.bfloat16)
    block = pl.BlockSpec((1, plan.grid_rows, plan.wide), lambda z, ids: (at + z, 0, 0))
    fspec = pl.BlockSpec((1, plan.grid_rows, plan.rows, LX), lambda z, ids: (z0 + at + z, 0, 0, 0))
    aliases = {1 + 2 + len(tabs) + i: i for i in range(len(prev))}
    return rows_call(
        kernel, "analyse_xy", ids, count, [field, ty, *tabs],
        [fspec, pick_block(ty, 0)] + [whole_block(t) for t in tabs],
        [out, out], [block, block],
        [pltpu.VMEM((2 * MY, plan.grid_rows, LX), jnp.bfloat16)], 2.8 * count, [*prev, *after], aliases, 52,
    )


def field_pass(plan, ids, tiles, windows, own, other, field, point, ty, ty_inv, xi, z0, zc, at, count, after, prev, cot=None, bias=None):
    first = cot is not None
    tabs = [far(jnp.asarray(t[3])) for t in tiles] if first else []
    block_rows = 4 * WIDTH
    half = plan.rows // 2
    pair = 2 * GROUP
    at0 = at

    def kernel(ids_ref, *refs):
        refs = list(refs)
        s_refs = (refs.pop(0), refs.pop(0))
        f, point_ref, tyi, xi_ref = refs.pop(0), refs.pop(0), refs.pop(0), refs.pop(0)
        if first:
            c_ref, bias_ref, ty_ref = refs.pop(0), refs.pop(0), refs.pop(0)
            tables = [refs.pop(0) for _ in tabs]
            g_out = refs.pop(0)
            outs = (refs.pop(0), refs.pop(0))
            us = refs.pop()
        else:
            g_out = refs.pop(0)
        ws, pre, mix = refs

        @pl.when(pl.program_id(0) == 0)
        def _():
            mix[...] = repeat_rows(point_ref[...], half)

        z = at0 + pl.program_id(0) if WHOLE else 0
        for h in range(plan.col):
            for k in range(plan.ky_half):
                low, high = windows[k]
                w = dot(s_refs[h][z, :, low:high], xi_ref[k, : high - low])
                ws[h * plan.ky_half + k] = w[:, :LX]
                ws[MY + h * plan.ky_half + k] = w[:, LX:]

        def block(i, carry):
            base = pl.multiple_of(i * block_rows, block_rows)
            rhs = lambda g: ws[:, pl.ds(g, GROUP), :].reshape(2 * MY * GROUP, LX).astype(jnp.bfloat16)

            def pointwise(t):
                v = f[0, pl.ds(base + t * WIDTH, WIDTH)]
                a = v[:, :half].reshape(WIDTH * half, LX)
                b = v[:, half:].reshape(WIDTH * half, LX)
                o = dot(mix[...], jnp.concatenate([a, b], 1))
                at = t * WIDTH
                pre[at : at + WIDTH, :half] = o[:, :LX].reshape(WIDTH, half, LX)
                pre[at : at + WIDTH, half:] = o[:, LX:].reshape(WIDTH, half, LX)

            def inverse(q):
                g = pl.multiple_of(base + q * pair, GROUP)
                o = dot(tyi[...], jnp.concatenate([rhs(g), rhs(g + GROUP)], 1))
                return o[:, :LX].reshape(GROUP, plan.rows, LX), o[:, LX:].reshape(GROUP, plan.rows, LX)

            def finish(q, parts):
                for m in range(pair):
                    at = q * pair + m
                    v = pre[at] + parts[m // GROUP][m % GROUP]
                    if first:
                        c = c_ref[0, base + at].astype(jnp.float32)
                        v = c * slope_of(v + bias_ref[at % WIDTH])
                    g_out[0, base + at] = v.astype(jnp.bfloat16)

            count = block_rows // pair
            for t in range(block_rows // WIDTH):
                pointwise(t)
            parts = inverse(0)
            for q in range(count):
                following = inverse(q + 1) if q + 1 < count else None
                finish(q, parts)
                parts = following
                if first:
                    spread_y(plan, g_out, base + q * pair, pair, ty_ref[...], us)
            return carry

        lax.fori_loop(0, plan.grid_rows // block_rows, block, 0)
        if first:
            gather_x(plan, tiles, us, tables, outs)

    cell = (1, plan.grid_rows, plan.rows, LX)
    local = pl.BlockSpec(cell, lambda z, ids: (at + z, 0, 0, 0))
    placed = pl.BlockSpec(cell, lambda z, ids: (z0 + at + z, 0, 0, 0))
    sblock = pl.BlockSpec((1, plan.grid_rows, plan.wide), lambda z, ids: (at + z, 0, 0))
    scratch = [
        pltpu.VMEM((2 * MY, plan.grid_rows, LX), jnp.float32),
        pltpu.VMEM((block_rows, plan.rows, LX), jnp.float32),
        pltpu.VMEM((WIDTH * half, WIDTH * half), jnp.bfloat16),
    ]
    inputs = [own, other, field, point, ty_inv, xi]
    kept = whole_block(own) if WHOLE else sblock
    specs = [kept, kept, placed if first else local, whole_block(point), pick_block(ty_inv, 0), whole_block(xi)]
    if first:
        inputs += [cot, bias, ty, *tabs]
        specs += [placed, pl.BlockSpec(memory_space=pltpu.SMEM), pick_block(ty, 0)]
        specs += [whole_block(t) for t in tabs]
        spec = jax.ShapeDtypeStruct((zc, plan.grid_rows, plan.wide), jnp.bfloat16)
        gout = jax.ShapeDtypeStruct((zc,) + cell[1:], jnp.bfloat16)
        shapes, out_specs, us, name = [gout, spec, spec], [local, sblock, sblock], 9.6, "slope_pass"
        scratch.append(pltpu.VMEM((2 * MY, plan.grid_rows, LX), jnp.bfloat16))
    else:
        shapes, out_specs = [jax.ShapeDtypeStruct((plan.depth,) + cell[1:], jnp.bfloat16)], [placed]
        us, name = 4.4, "input_pass"
    aliases = {1 + len(inputs) + i: i for i in range(len(prev))}
    return rows_call(
        kernel, name, ids, count, inputs, specs, shapes, out_specs, scratch, us * count, [*prev, *after], aliases, 42
    )


def time_forward(plan, ids, own, other, table, after):
    zc = own.shape[0]

    def kernel(ids_ref, a_ref, b_ref, m_ref, keep, send):
        for z in range(zc):
            a = a_ref[z, :, : plan.lanes].astype(jnp.float32) + b_ref[z, :, : plan.lanes].astype(jnp.float32)
            at = jnp.transpose(a).astype(jnp.bfloat16)
            p = dot(at, m_ref[...]).reshape(plan.ky_half, 2, MX, 4 * LANE)
            re = p[:, 0, :, : 2 * LANE] - p[:, 1, :, 2 * LANE :]
            im = p[:, 0, :, 2 * LANE :] + p[:, 1, :, : 2 * LANE]
            re, im = (v.reshape(plan.gz, plan.owned, 2 * LANE).astype(jnp.bfloat16) for v in (re, im))
            keep[:, z, :, :LANE], keep[:, z, :, LANE:] = re[..., :LANE], im[..., :LANE]
            send[:, z, :, :LANE], send[:, z, :, LANE:] = re[..., LANE:], im[..., LANE:]

    out = jax.ShapeDtypeStruct((plan.gz, zc, plan.owned, 2 * LANE), jnp.bfloat16)
    return rows_call(
        kernel, "time_forward", ids, 1, [own, other, table],
        [whole_block(own), whole_block(other), pick_block(table, 2)], [out, out], [whole_block(out)] * 2, [], 0.4 * zc, after,
    )


def time_inverse(plan, ids, keep, got, table, after):
    zc = keep[0].shape[1]
    gp = plan.grid_rows_padded()
    flat = [*keep, *got]

    def kernel(ids_ref, *refs):
        ins, m_ref, out = refs[: len(flat)], refs[-2], refs[-1]
        for z in range(zc):
            stacked = lambda rs: jnp.concatenate([r[:, z].reshape(-1, 2 * LANE) for r in rs], 0)
            a, b = stacked(ins[: len(keep)]), stacked(ins[len(keep) :])
            o = dot(jnp.concatenate([a, b], 1), m_ref[...]).reshape(plan.ky_half, 1, MX, 2 * gp)
            o = jnp.concatenate([o[..., :gp], o[..., gp:]], 1).reshape(plan.lanes, gp)
            out[z, :, : plan.lanes] = jnp.transpose(o)[: plan.grid_rows].astype(jnp.bfloat16)

    out = jax.ShapeDtypeStruct((zc, plan.grid_rows, plan.wide), jnp.bfloat16)
    return rows_call(
        kernel, "time_inverse", ids, 1, [*flat, table],
        [whole_block(a) for a in flat] + [pick_block(table, 2)],
        [out], [whole_block(out)], [], 0.4 * zc, after,
    )[0]


def depth_forward(plan, ids, pieces, table):
    flat = [p for chunk in pieces for p in chunk]
    n = len(flat)
    zc = flat[0].shape[1]
    octets = plan.owned // GROUP
    count = plan.gz * plan.depth

    def kernel(ids_ref, *refs):
        ins, m_ref, keep, send, buf, out = refs[:n], refs[n], refs[n + 1], refs[n + 2], refs[n + 3], refs[n + 4]
        at = 0
        for ref in ins:
            for k in range(ref.shape[0]):
                c, shift = at // plan.gz, at % plan.gz
                first = shift * plan.depth + c * zc
                buf[first : first + zc] = ref[k].astype(jnp.float32)
                at += 1
        for o in range(octets):
            x = buf[:, o * GROUP : (o + 1) * GROUP, :].reshape(count * GROUP, 2 * LANE)
            x = jnp.concatenate([x[:, :LANE], x[:, LANE:]], 0).astype(jnp.bfloat16)
            y = dot(m_ref[...], x).reshape(plan.ta, 2, plan.kz, GROUP, LANE)
            for h in range(plan.ta):
                for s in range(2):
                    out[h, :, o * GROUP : (o + 1) * GROUP, s * LANE : (s + 1) * LANE] = y[h, s]
        keep[...] = out[0].astype(jnp.bfloat16)
        send[...] = out[1].astype(jnp.bfloat16)

    shape = jax.ShapeDtypeStruct((plan.kz, plan.owned, 2 * LANE), jnp.bfloat16)
    return rows_call(
        kernel, "depth_forward", ids, 1, [*flat, table], [whole_block(a) for a in flat] + [pick_block(table, 1)],
        [shape, shape], [pl.BlockSpec(shape.shape, lambda *i: (0, 0, 0))] * 2,
        [
            pltpu.VMEM((count, plan.owned, 2 * LANE), jnp.float32),
            pltpu.VMEM((plan.ta, plan.kz, plan.owned, 2 * LANE), jnp.float32),
        ], 1.4,
    )


def depth_inverse(plan, ids, keep, got, table, chunk, chunks, after):
    octets = plan.owned // GROUP
    zc = plan.depth // chunks
    cut = plan.gz if SHIFTS else 1

    def kernel(ids_ref, a_ref, b_ref, m_ref, *refs):
        outs, buf, out = refs[:-2], refs[-2], refs[-1]
        buf[0] = a_ref[...].astype(jnp.float32)
        buf[1] = b_ref[...].astype(jnp.float32)
        m = m_ref[...].reshape(2 * plan.gz, plan.depth * GROUP, -1)
        m = m[:, chunk * zc * GROUP : (chunk + 1) * zc * GROUP].reshape(2 * plan.gz * zc * GROUP, -1)
        for o in range(octets):
            rows = slice(o * GROUP, (o + 1) * GROUP)
            x = [
                buf[h, :, rows, s * LANE : (s + 1) * LANE].reshape(plan.kz * GROUP, LANE)
                for h in range(plan.ta)
                for s in range(2)
            ]
            y = dot(m, jnp.concatenate(x, 0).astype(jnp.bfloat16))
            y = y.reshape(2, plan.gz * zc, GROUP, LANE)
            for s in range(2):
                out[:, rows, s * LANE : (s + 1) * LANE] = y[s]
        for k in range(plan.gz):
            outs[k % cut][k // cut] = out[k * zc : (k + 1) * zc].astype(jnp.bfloat16)

    shape = jax.ShapeDtypeStruct((plan.gz // cut, zc, plan.owned, 2 * LANE), jnp.bfloat16)
    return rows_call(
        kernel, "depth_inverse", ids, 1, [keep, got, table],
        [whole_block(keep), whole_block(got), pick_block(table, 1)],
        [shape] * cut, [pl.BlockSpec(shape.shape, lambda *i: (0, 0, 0, 0))] * cut,
        [
            pltpu.VMEM((plan.ta, plan.kz, plan.owned, 2 * LANE), jnp.float32),
            pltpu.VMEM((plan.gz * zc, plan.owned, 2 * LANE), jnp.float32),
        ], 1.0, after,
    )


def swap_pairs(v):
    n = v.shape[0]
    even = lax.rem(lax.broadcasted_iota(jnp.int32, v.shape, 0), 2) == 0
    return jnp.where(even, -pltpu.roll(v, n - 1, 0), pltpu.roll(v, 1, 0))


def to_comm(plan, rows_ref, perm, keep, send):
    o = dot(jnp.transpose(rows_ref[...]).astype(jnp.bfloat16), perm[...]).astype(jnp.bfloat16)
    keep[0] = o[:, : 2 * LANE]
    send[0] = o[:, 2 * LANE :]


def mode_specs(plan):
    mode_rows = MT * WIDTH * WIDTH * 2
    half = pl.BlockSpec((1, plan.owned, 2 * LANE), lambda k, ids: (k, 0, 0))
    weights = pl.BlockSpec((1, mode_rows, plan.owned), lambda k, ids: (k, 0, 0))
    return half, weights, mode_rows


def mix_modes(plan, ids, spec, weights, perm, unit):
    half, wspec, mode_rows = mode_specs(plan)
    per_t = WIDTH * WIDTH * 2
    wide = 2 * WIDTH

    def kernel(ids_ref, a_ref, b_ref, w_ref, perm_ref, unit_ref, keep, send, xs, ms):
        x = jnp.concatenate([a_ref[0], b_ref[0]], 1)
        xs[...] = dot_nt(unit_ref[...], x)

        def step(q, carry):
            h = q // plan.kt
            kt = q - h * plan.kt
            at = lax.rem(q + ids_ref[2] * plan.kt, MT)
            row = h * 2 * LANE + kt * WIDTH
            s1 = jnp.zeros((wide, plan.owned), jnp.float32)
            s2 = jnp.zeros((wide, plan.owned), jnp.float32)
            for i in range(0, WIDTH, 2):
                w = w_ref[0, pl.ds(pl.multiple_of(at * per_t + i * wide, 2 * wide), 2 * wide), :].astype(jnp.float32)
                for j in range(2):
                    wi = w[j * wide : (j + 1) * wide]
                    s1 += xs[pl.ds(row + i + j, 1), :] * wi
                    s2 += xs[pl.ds(row + LANE + i + j, 1), :] * wi
            ms[pl.ds(pl.multiple_of(q * wide, 8), wide), :] = s1 + swap_pairs(s2)
            return carry

        lax.fori_loop(0, MT, step, 0, unroll=UNROLL)
        to_comm(plan, ms, perm_ref, keep, send)

    shape = jax.ShapeDtypeStruct((plan.kz, plan.owned, 2 * LANE), jnp.bfloat16)
    return rows_call(
        kernel, "mix_modes", ids, plan.kz, [*spec, weights, perm, unit],
        [half, half, wspec, whole_block(perm), whole_block(unit)],
        [shape, shape], [half, half],
        [
            pltpu.VMEM((2 * plan.ta * LANE, plan.owned), jnp.float32),
            pltpu.VMEM((MT * wide, plan.owned), jnp.float32),
        ], 17.0, vmem=46,
    )


def back_modes(plan, ids, grad, weights, perm):
    half, wspec, mode_rows = mode_specs(plan)
    per_t = WIDTH * WIDTH * 2
    wide = 2 * WIDTH

    def kernel(ids_ref, a_ref, b_ref, w_ref, perm_ref, keep, send, gs, ms):
        gs[...] = dot_nt(perm_ref[...], jnp.concatenate([a_ref[0], b_ref[0]], 1))

        def step(q, carry):
            at = lax.rem(q + ids_ref[2] * plan.kt, MT)
            g = gs[pl.ds(pl.multiple_of(q * wide, 8), wide), :]
            g2 = -swap_pairs(g)
            rows = []
            for i in range(0, WIDTH, 2):
                w = w_ref[0, pl.ds(pl.multiple_of(at * per_t + i * wide, 2 * wide), 2 * wide), :].astype(jnp.float32)
                for j in range(2):
                    wi = w[j * wide : (j + 1) * wide]
                    rows.append(jnp.sum(g * wi, 0, keepdims=True))
                    rows.append(jnp.sum(g2 * wi, 0, keepdims=True))
            ms[pl.ds(pl.multiple_of(q * wide, 8), wide), :] = jnp.concatenate(rows, 0)
            return carry

        lax.fori_loop(0, MT, step, 0, unroll=UNROLL)
        to_comm(plan, ms, perm_ref, keep, send)

    shape = jax.ShapeDtypeStruct((plan.kz, plan.owned, 2 * LANE), jnp.bfloat16)
    return rows_call(
        kernel, "back_modes", ids, plan.kz, [*grad, weights, perm],
        [half, half, wspec, whole_block(perm)],
        [shape, shape], [half, half],
        [pltpu.VMEM((MT * wide, plan.owned), jnp.float32)] * 2, 20.0, vmem=46,
    )


def weight_modes(plan, ids, spec, grad, perm, unit, k0, count, full, after):
    _, _, mode_rows = mode_specs(plan)
    half = pl.BlockSpec((1, plan.owned, 2 * LANE), lambda k, ids: (k0 + k, 0, 0))
    wspec = pl.BlockSpec((1, mode_rows, plan.owned), lambda k, ids: (k0 + k, 0, 0))
    per_t = WIDTH * WIDTH * 2
    wide = 2 * WIDTH

    def kernel(ids_ref, xa, xb, ga, gb, perm_ref, unit_ref, out, xs, gs):
        xs[...] = dot_nt(unit_ref[...], jnp.concatenate([xa[0], xb[0]], 1))
        gs[...] = dot_nt(perm_ref[...], jnp.concatenate([ga[0], gb[0]], 1))

        def step(q, carry):
            h = q // plan.kt
            kt = q - h * plan.kt
            at = lax.rem(q + ids_ref[2] * plan.kt, MT)
            row = h * 2 * LANE + kt * WIDTH
            g = gs[pl.ds(pl.multiple_of(q * wide, 8), wide), :]
            g2 = -swap_pairs(g)
            for i in range(0, WIDTH, 2):
                two = [
                    xs[pl.ds(row + i + j, 1), :] * g + xs[pl.ds(row + LANE + i + j, 1), :] * g2
                    for j in range(2)
                ]
                rows = pl.ds(pl.multiple_of(at * per_t + i * wide, 2 * wide), 2 * wide)
                out[0, rows, :] = jnp.concatenate(two, 0).astype(jnp.bfloat16)
            return carry

        lax.fori_loop(0, MT, step, 0, unroll=UNROLL)

    shape = jax.ShapeDtypeStruct((plan.kz, mode_rows, plan.owned), jnp.bfloat16)
    return rows_call(
        kernel, "weight_modes", ids, count, [*spec, *grad, perm, unit],
        [half, half, half, half, whole_block(perm), whole_block(unit)],
        [shape], [wspec],
        [
            pltpu.VMEM((2 * plan.ta * LANE, plan.owned), jnp.float32),
            pltpu.VMEM((MT * wide, plan.owned), jnp.float32),
        ], 1.8 * count, [*([] if full is None else [full]), *after], {} if full is None else {7: 0}, 46,
    )[0]


def direct_device(plan, field, cotangent, spectral_weight, point_weight, point_bias):
    gz_at, ta_at, col_at = (lax.axis_index(a) for a in ("gz", "ta", "col"))
    chunks = CHUNKS
    zc = plan.depth // chunks
    ids = jnp.stack([gz_at * plan.col + col_at, gz_at * plan.ta + ta_at, ta_at]).astype(jnp.int32)
    y_table = plan.y_tables()
    ty, ty_inv = far(jnp.asarray(y_table)), far(jnp.asarray(np.swapaxes(y_table, 1, 2).copy()))
    tiles = plan.x_tiles()
    windows, xi = plan.x_windows()
    xi = far(jnp.asarray(xi))
    zf, zi = (jnp.asarray(t) for t in plan.z_tables())
    t_fwd, t_inv = (jnp.asarray(t) for t in plan.t_tables(False))
    tw_fwd, tw_inv = (jnp.asarray(t) for t in plan.t_tables(True))
    perm = jnp.asarray(plan.pair_rows())
    unit = jnp.asarray(bf16(np.eye(2 * plan.ta * LANE)))
    flat = (plan.depth, plan.grid_rows, plan.rows, LX)
    field, cotangent = field.reshape(flat), cotangent.reshape(flat)
    weights = jnp.transpose(spectral_weight, (0, 1, 4, 5, 3, 2))
    weights = weights.reshape(plan.kz, MT * WIDTH * WIDTH * 2, plan.owned)

    def swap(a, axis):
        return lax.ppermute(a, axis, [(0, 1), (1, 0)])

    def spread(blocks, sign):
        if not SHIFTS:
            return [lax.all_to_all(blocks[0], "gz", 0, 0, tiled=True)]
        moved = [blocks[0]]
        for k in range(1, plan.gz):
            moved.append(lax.ppermute(blocks[k], "gz", [(d, (d + sign * k) % plan.gz) for d in range(plan.gz)]))
        return moved

    def outward(own, other, table, before):
        after = [before[-1]] if before and QUEUE_OUT else []
        keep, send = time_forward(plan, ids, own, swap(other, "col"), table, after)
        total = (keep.astype(jnp.float32) + swap(send, "ta").astype(jnp.float32)).astype(jnp.bfloat16)
        blocks = [total[k : k + 1] for k in range(plan.gz)] if SHIFTS else [total]
        return spread(blocks, 1), total

    def collect(pieces):
        keep, send = depth_forward(plan, ids, pieces, zf)
        return keep, swap(send, "ta")

    def inward(keep, send, beside=None):
        out = []
        got = swap(send, "ta")
        for n in range(chunks):
            after = out[-1][0] if out and QUEUE_IN else []
            if n == 1 and beside is not None and EARLY:
                after = [*after, *beside(blocks[:1])]
            blocks = depth_inverse(plan, ids, keep, got, zi, n, chunks, after)
            mine = spread(blocks, -1)
            if len(mine) > 1:
                mine = [jnp.concatenate(mine, 0)]
            out.append((mine, [swap(m, "ta") for m in mine]))
        return out

    def planes(pieces, table, after):
        own = time_inverse(plan, ids, *pieces, table, after)
        return own, swap(own, "col")

    sub = zc // PARTS
    pieces, sent = [], []
    for n in range(chunks):
        made = []
        for m in range(PARTS):
            after = [sent[n - 1]] if n and m == 1 else []
            made = analyse_xy(plan, ids, tiles, field, ty, n * zc, zc, m * sub, sub, after, made)
        moved, send = outward(*made, t_fwd, sent)
        pieces.append(moved)
        sent.append(send)
    spec = collect(pieces)
    mixed = mix_modes(plan, ids, spec, weights, perm, unit)
    arrived = inward(*mixed)
    pieces, gprime, sent = [], [], []
    for n in range(chunks):
        made = []
        plane = planes(arrived[n], tw_inv, [far(gprime[-1])] if n and ORDERED else [])
        for m in range(PARTS):
            after = [sent[n - 1]] if n and m == 1 else []
            made = field_pass(
                plan, ids, tiles, windows, *plane, field, point_weight.T, ty, ty_inv, xi,
                n * zc, zc, m * sub, sub, after, made, cot=cotangent, bias=point_bias,
            )
        g, own, other = made
        gprime.append(g)
        moved, send = outward(own, other, tw_fwd, sent)
        pieces.append(moved)
        sent.append(send)
    grad = collect(pieces)
    back = back_modes(plan, ids, grad, weights, perm)
    weight_grad = None

    def beside(first):
        nonlocal weight_grad
        at = 0
        for count in WEIGHT_SIZES:
            weight_grad = weight_modes(plan, ids, spec, grad, perm, unit, at, count, weight_grad, first if at == 0 else [])
            at += count
        return [far(weight_grad)]

    arrived = inward(*back, beside)
    if not EARLY:
        beside([])
    made = []
    for n in range(chunks):
        after = [far(weight_grad)] if n == 0 and not EARLY else []
        after += [far(made[0])] if n and LAST_ORDERED else []
        plane = planes(arrived[n], t_inv, after)
        made = field_pass(
            plan, ids, tiles, windows, *plane, gprime[n], point_weight, ty, ty_inv, xi, n * zc, zc, 0, zc, [], made
        )
    input_grad = made[0].reshape(plan.depth, plan.steps, WIDTH, plan.rows, LX)
    weight_grad = weight_grad.reshape(plan.kz, MT, WIDTH, WIDTH, 2, plan.owned)
    return input_grad, jnp.transpose(weight_grad, (0, 1, 5, 4, 2, 3))


def per_device(mesh, field, cotangent, spectral_weight, point_weight, point_bias):
    args = (field, cotangent, spectral_weight, point_weight, point_bias)
    depth, steps, _, rows, _ = field.shape
    plan = Plan(mesh, depth, steps, rows)
    fits = (
        plan.col == 2
        and plan.ta == 2
        and plan.owned % MX == 0
        and plan.owned % GROUP == 0
        and steps % 4 == 0
        and rows == 32
        and plan.kt * WIDTH <= LANE
        and depth % CHUNKS == 0
        and plan.kz == sum(WEIGHT_SIZES)
    )
    if fits:
        return direct_device(plan, *args)
    return general_device(*args)


def solution(mesh):
    placed = (
        P(("groups", "gz"), "ta", None, "col", None),
        P(("groups", "gz"), "ta", None, "col", None),
        P("ta", None, ("gz", "col"), None, None, None),
        P(),
        P(),
    )
    return jax.shard_map(
        functools.partial(per_device, mesh),
        mesh=mesh,
        in_specs=placed,
        out_specs=(
            P(("groups", "gz"), "ta", None, "col", None),
            P(("groups", "ta"), None, ("gz", "col"), None, None, None),
        ),
        check_vma=False,
    )
```
